512 devices in a mesh: team: 8 (over z), blk: 16 (over y_hi, x), head: 4 (over y_lo, core).
Axes of the slice: x: 4, y: 8 (y_hi: 4, y_lo: 2; y = y_hi * 2 + y_lo), z: 8, core: 2. Of those that a mesh axis runs over, the one named last changes fastest.
Arguments:
- queries: bfloat16 [4096, 8, 8, 128], P('blk', 'head', 'team'), may hold values from -40 to 40
- features: bfloat16 [4096, 8192], P('blk', ('team', 'head')), may hold values from -6 to 6
- adapter_down: bfloat16 [4, 8192, 64], P(None, ('team', 'head')), may hold values from -0.0625 to 0.0625
- adapter_key_up: bfloat16 [4, 64, 8, 128], P(None, None, 'head'), may hold values from -0.75 to 0.75
- adapter_value_up: bfloat16 [4, 64, 8, 128], P(None, None, 'head'), may hold values from -0.75 to 0.75
- base_key: bfloat16 [4096, 8, 128], P('blk', 'head'), may hold values from -6 to 6
- base_value: bfloat16 [4096, 8, 128], P('blk', 'head'), may hold values from -24 to 24
- prefix_key: bfloat16 [8192, 8, 128], P('blk', 'head'), may hold values from -7 to 7
- prefix_value: bfloat16 [8192, 8, 128], P('blk', 'head'), may hold values from -24 to 24
- adapter_ids: int32 [16], replicated, may hold values from 0 to 3
- block_order: int32 [16], replicated, may hold values from 0 to 63
Outputs:
- attended: bfloat16 [4096, 8, 8, 128], P('blk', 'head', 'team')
The draws below stay inside these ranges and needn't reach their ends.
All inputs are finite; a program needn't handle non-finite values.
Results may differ from the reference program's by a relative error of at most 0.011.
Values may be sent and summed in bfloat16 or wider, within the bound.
A program may use at most 64 MiB of HBM per device.

```python
import math
import jax
import jax.numpy as jnp
from jax import lax

D = 8192
KVH = 8
GROUP = 8
HD = 128
RANK = 64
ADAPTERS = 4
Q_DEV = 256
BLOCKS = 16
NEW = 4096
PREFIX = 8192


def drawn_draw(key):
    query_key, key_key = jax.random.split(jax.random.fold_in(key, 7301), 2)
    query_vals = jnp.clip(2.0 * jax.random.normal(query_key, (NEW, KVH, GROUP, HD), jnp.float32), -12.0, 12.0)
    key_vals = jnp.clip(jax.random.normal(key_key, (PREFIX, KVH, HD), jnp.float32), -6.0, 6.0)
    return (query_vals, key_vals)


def draw_queries(key, part):
    return drawn_draw(key)[0].astype(jnp.bfloat16)


def draw_prefix_key(key, part):
    return drawn_draw(key)[1].astype(jnp.bfloat16)


def plant(result, rng, least, largest):
    shape = result.shape
    index_at = [jax.random.randint(jax.random.fold_in(rng, axis), (), 0, shape[axis]) for axis in range(len(shape))]
    result = result.at[tuple(index_at)].set(least)
    longest = shape.index(max(shape))
    index_at[longest] = (index_at[longest] + 1) % shape[longest]
    return result.at[tuple(index_at)].set(largest)


def levels(rng, shape, cuts, least, top_value):
    loudness, own = 1.0, jax.random.fold_in(rng, 6)
    for dim, blocks in cuts:
        draws = jnp.exp(jax.random.uniform(jax.random.fold_in(own, dim), (blocks,), jnp.float32, least / len(cuts), top_value / len(cuts)))
        loudness = loudness * jnp.repeat(draws, shape[dim] // blocks).reshape([-1 if axis == dim else 1 for axis in range(len(shape))])
    return loudness


def centred(own_key, extent, spread, bound, shards=(), kind=jnp.bfloat16):
    values = spread * jax.random.normal(own_key, extent, jnp.float32)
    if shards:
        values = values * levels(own_key, extent, shards, -0.22, 0.18)
    return jnp.clip(values, -bound, bound).astype(kind)


def setup_inputs(seed: int = 0) -> dict:
    keys = jax.random.split(jax.random.key(seed), 12)
    queries = draw_queries(jax.random.fold_in(keys[11], 71), 0)
    features = centred(keys[1], (NEW, D), 1.0, 6.0, ((0, 16), (1, 32)))
    adapter_down = centred(keys[2], (ADAPTERS, D, RANK), D ** -0.5, 0.0625, ((1, 32),))
    adapter_key_up = centred(keys[3], (ADAPTERS, RANK, KVH, HD), RANK ** -0.5, 0.75, ((2, 4),))
    adapter_value_up = centred(keys[4], (ADAPTERS, RANK, KVH, HD), RANK ** -0.5, 0.75, ((2, 4),))
    base_key = centred(keys[5], (NEW, KVH, HD), 1.0, 6.0, ((0, 16), (1, 4)))
    base_value = centred(keys[6], (NEW, KVH, HD), 4.0, 24.0, ((0, 16), (1, 4)))
    prefix_key = draw_prefix_key(jax.random.fold_in(keys[11], 71), 0)
    prefix_value = centred(keys[8], (PREFIX, KVH, HD), 4.0, 24.0, ((0, 16), (1, 4)))
    adapter_ids = plant(jax.random.randint(keys[9], (BLOCKS,), 0, ADAPTERS), jax.random.fold_in(keys[9], 1), 0, ADAPTERS - 1).astype(jnp.int32)
    block_order = plant(jax.random.randint(keys[10], (BLOCKS,), 0, 4 * BLOCKS), jax.random.fold_in(keys[10], 1), 0, (4 * BLOCKS) - 1).astype(jnp.int32)
    return dict(queries=queries, features=features, adapter_down=adapter_down, adapter_key_up=adapter_key_up, adapter_value_up=adapter_value_up, base_key=base_key, base_value=base_value, prefix_key=prefix_key, prefix_value=prefix_value, adapter_ids=adapter_ids, block_order=block_order)


NEG_FILL = -1e+30

def reference(queries, features, adapter_down, adapter_key_up, adapter_value_up, base_key, base_value, prefix_key, prefix_value, adapter_ids, block_order):
    block_count = block_order.shape[0]
    highest = lax.Precision.HIGHEST
    token_index = jnp.arange(NEW, dtype=jnp.int32)
    query_pos = PREFIX + block_order[token_index // Q_DEV] * Q_DEV + token_index % Q_DEV
    key_pos = jnp.concatenate([jnp.arange(PREFIX, dtype=jnp.int32), query_pos])
    down_rows = adapter_down[adapter_ids].astype(jnp.float32)
    grouped = features.reshape(block_count, Q_DEV, D).astype(jnp.float32)
    latent = jnp.einsum('btd,bdr->btr', grouped, down_rows, precision=highest)
    latent_wide = lax.optimization_barrier(latent.astype(jnp.bfloat16)).astype(jnp.float32)

    def expand(up_table, base_rows):
        up_rows = up_table[adapter_ids].reshape(block_count, RANK, KVH * HD).astype(jnp.float32)
        delta = jnp.einsum('btr,bre->bte', latent_wide, up_rows, precision=highest).reshape(NEW, KVH, HD)
        return (base_rows.astype(jnp.float32) + delta).astype(jnp.bfloat16)
    key_rows = jnp.concatenate([prefix_key, expand(adapter_key_up, base_key)], axis=0)
    value_rows = jnp.concatenate([prefix_value, expand(adapter_value_up, base_value)], axis=0)
    score_scale = 1.0 / math.sqrt(HD)

    def one_head(head_index):
        head_keys = lax.dynamic_index_in_dim(key_rows, head_index, 1, keepdims=False).astype(jnp.float32)
        head_values = lax.dynamic_index_in_dim(value_rows, head_index, 1, keepdims=False).astype(jnp.float32)
        head_queries = lax.dynamic_index_in_dim(queries, head_index, 1, keepdims=False)

        def one_block(block_index):
            block_queries = lax.dynamic_slice_in_dim(head_queries, block_index * Q_DEV, Q_DEV, 0).astype(jnp.float32)
            block_pos = lax.dynamic_slice_in_dim(query_pos, block_index * Q_DEV, Q_DEV, 0)
            scores = jnp.einsum('tgd,sd->gts', block_queries, head_keys, precision=highest) * score_scale
            visible = key_pos[None, None, :] <= block_pos[None, :, None]
            scores = jnp.where(visible, scores, NEG_FILL)
            row_max = lax.optimization_barrier(jnp.max(scores, axis=-1, keepdims=True))
            weights = jnp.where(visible, jnp.exp(scores - row_max), 0.0)
            row_sum = lax.optimization_barrier(jnp.sum(weights, axis=-1))
            rounded = lax.optimization_barrier(weights.astype(jnp.bfloat16)).astype(jnp.float32)
            mixed = jnp.einsum('gts,sd->gtd', rounded, head_values, precision=highest)
            return (mixed / row_sum[..., None]).astype(jnp.bfloat16)
        return lax.map(one_block, jnp.arange(block_count, dtype=jnp.int32))
    stacked = lax.map(one_head, jnp.arange(KVH, dtype=jnp.int32))
    return stacked.transpose(1, 3, 0, 2, 4).reshape(NEW, KVH, GROUP, HD)
```

```python
import math

import jax
import jax.numpy as jnp
from jax import lax
from jax.experimental import pallas as pl
from jax.experimental.pallas import tpu as pltpu
from jax.sharding import PartitionSpec as P

MESH = pl.DeviceIdType.MESH
BF16 = jnp.bfloat16
F32 = jnp.float32

TEAM, XN, YN, HEADS = 8, 4, 4, 4
QN, HD, KV = 256, 128, 2
PRE, NEW = 64, 32
RANK = 64
LOG_SCALE = math.log2(math.e) / math.sqrt(HD)
FAR = 7
TAIL = 16
MSG = HD + TAIL
NT = (((1,), (1,)), ((), ()))


def spread(ref, rows, count):
    ref[0 : 2 * count, :] = rows.astype(F32)
    return [ref[pl.ds(head, count, stride=2), :] for head in range(KV)]


def kernel(
    ids_ref, order_ref, q_ref, feat_ref, down_ref, kup_ref, vup_ref, bk_ref, bv_ref, pk_ref, pv_ref,
    out_ref,
    stage, stage_base, wide, ups, base, lat_own, lat_recv, lat_sum, qbuf, kvp, kvn, vt, bias,
    scores_r, scores_l, sent, landed, local_sem, send_sem, recv_sem,
):
    team = lax.axis_index("team")
    blk = lax.axis_index("blk")
    head = lax.axis_index("head")
    yh, x = blk // XN, blk % XN

    def at_z(d):
        return {"team": (team + d + TEAM) % TEAM}

    def at_y(d):
        return {"blk": ((yh + d + YN) % YN) * XN + x}

    def at_x(d):
        return {"blk": yh * XN + (x + d + XN) % XN}

    def at_head(d):
        return {"head": (head + d) % HEADS}

    barrier = pltpu.get_barrier_semaphore()
    peers = (
        [at_z(d) for d in range(1, TEAM)]
        + [at_y(d) for d in range(1, YN)]
        + [at_x(1), at_x(-1)]
        + [at_head(d) for d in range(1, HEADS)]
    )
    for peer in peers:
        pl.semaphore_signal(barrier, inc=1, device_id=peer, device_id_type=MESH)

    used = [0]
    started = []

    def copy_to(src, dst, peer):
        index = used[0]
        used[0] += 1
        started.append(
            pltpu.make_async_remote_copy(
                src_ref=src, dst_ref=dst, send_sem=send_sem.at[index], recv_sem=recv_sem.at[index],
                device_id=peer, device_id_type=MESH,
            )
        )
        started[-1].start()
        return started[-1]

    prefix_rows = pl.ds(pl.multiple_of(team * (KV * PRE), KV * PRE), KV * PRE)
    base_rows = pl.ds(pl.multiple_of(team * (KV * NEW), KV * NEW), KV * NEW)
    local = [
        pltpu.make_async_copy(pk_ref.at[prefix_rows], stage.at[0], local_sem.at[0]),
        pltpu.make_async_copy(pv_ref.at[prefix_rows], stage.at[1], local_sem.at[1]),
        pltpu.make_async_copy(bk_ref.at[base_rows], stage_base.at[0], local_sem.at[2]),
        pltpu.make_async_copy(bv_ref.at[base_rows], stage_base.at[1], local_sem.at[3]),
    ]
    for copy in local:
        copy.start()

    chosen = ids_ref[blk]
    down = down_ref[chosen]
    partial = lax.dot_general(
        feat_ref[...], jnp.concatenate([down, down], axis=0), NT, preferred_element_type=F32
    )
    first_half = lax.broadcasted_iota(jnp.int32, (16, HD), 1) < RANK
    for member in range(TEAM):
        row = member * NEW
        lat_own[member] = jnp.where(
            first_half, partial[row : row + 16], partial[row + 16 : row + 32]
        )
    for h, rows in enumerate(spread(wide, q_ref[...], QN)):
        qbuf[0, h] = rows.astype(BF16)
    for kind in range(2):
        local[kind].wait()
        for h, rows in enumerate(spread(wide, stage[kind], PRE)):
            kvp[2 * kind + h, 0, 0] = rows.astype(BF16)

    pl.semaphore_wait(barrier, len(peers))

    z_lat = [
        copy_to(lat_own.at[(team + d) % TEAM], lat_recv.at[d], at_z(d)) for d in range(1, TEAM)
    ]

    q_right, q_left = {}, {}

    def send_q(step, h):
        if step:
            q_right[step, h].wait_recv()
        src = step
        dst = FAR if step == 3 else step + 1
        q_right[step + 1, h] = copy_to(qbuf.at[src, h], qbuf.at[dst, h], at_z(1))
        if step:
            q_left[step, 1 - h].wait_recv()
        src = 3 + step if step else 0
        dst = FAR if step == 3 else 4 + step
        q_left[step + 1, 1 - h] = copy_to(qbuf.at[src, 1 - h], qbuf.at[dst, 1 - h], at_z(-1))

    class Rows:
        def __init__(self, buf):
            self.buf = buf
            self.y, self.right, self.left, self.far = {}, {}, {}, {}

        def send_y(self):
            for d in (1, 3, 2):
                self.y[d] = copy_to(self.buf.at[:, 0, 0], self.buf.at[:, 0, d], at_y(d))

        def send_x(self, d):
            if d:
                self.y[d].wait_recv()
            self.right[d] = copy_to(self.buf.at[:, 0, d], self.buf.at[:, 1, d], at_x(1))
            self.left[d] = copy_to(self.buf.at[:, 0, d], self.buf.at[:, 2, d], at_x(-1))

        def pass_x(self, d):
            keys, values = pl.ds(0, 2), pl.ds(2, 2)
            self.right[d].wait_recv()
            self.far[0, d] = copy_to(self.buf.at[keys, 1, d], self.buf.at[keys, 3, d], at_x(1))
            self.left[d].wait_recv()
            self.far[1, d] = copy_to(self.buf.at[values, 2, d], self.buf.at[values, 3, d], at_x(-1))

    prefix, fresh = Rows(kvp), Rows(kvn)

    send_q(0, 1)
    send_q(0, 0)
    prefix.send_x(0)
    prefix.send_y()

    for kind, table in enumerate((kup_ref, vup_ref)):
        for h, rows in enumerate(spread(wide, table[chosen], RANK)):
            ups[2 * kind + h] = jnp.concatenate([rows, rows], axis=0).astype(BF16)
    for kind in range(2):
        local[2 + kind].wait()
        for h, rows in enumerate(spread(wide, stage_base[kind], NEW)):
            base[2 * kind + h] = rows
    token = order_ref[blk] * QN + lax.broadcasted_iota(jnp.int32, (NEW, QN), 1)
    within = team * NEW + lax.broadcasted_iota(jnp.int32, (NEW, QN), 0)
    for column, dx in enumerate((0, 1, -1, 2)):
        for d in range(YN):
            owner = ((yh - d + YN) % YN) * XN + (x - dx + XN) % XN
            hidden = order_ref[owner] * QN + within > token
            bias[pl.ds((column * YN + d) * NEW, NEW), :] = jnp.where(hidden, -1e30, 0.0)
    for h in range(KV):
        vt[h, HD:MSG, :] = jnp.ones((TAIL, TEAM * (PRE + NEW) * 2), BF16)
    is_first = lax.broadcasted_iota(jnp.int32, (TAIL, QN), 0) == 0
    for side in range(2):
        for slot in range(2):
            landed[side, slot, 0:HD, :] = jnp.zeros((HD, QN), BF16)
            landed[side, slot, HD:MSG, :] = jnp.where(is_first, -1e30, 0.0).astype(BF16)

    for copy in z_lat:
        copy.wait_recv()
    total = lat_own[team]
    for d in range(1, TEAM):
        total = total + lat_recv[d]
    lat_sum[0] = total
    head_lat = [copy_to(lat_sum.at[0], lat_sum.at[d], at_head(d)) for d in range(1, HEADS)]

    prefix.pass_x(0)
    send_q(1, 1)
    prefix.send_x(1)
    prefix.send_x(3)

    for copy in head_lat:
        copy.wait_recv()
    latent = lat_sum[0] + lat_sum[1] + lat_sum[2] + lat_sum[3]
    latent = jnp.concatenate(
        [jnp.where(first_half, latent, 0.0), jnp.where(first_half, 0.0, latent)], axis=0
    ).astype(BF16)
    for part in range(2 * KV):
        delta = jnp.dot(latent, ups[part], preferred_element_type=F32)
        kvn[part, 0, 0] = (base[part] + delta).astype(BF16)
    fresh.send_y()
    fresh.send_x(0)

    send_q(1, 0)
    prefix.send_x(2)
    prefix.pass_x(1)
    prefix.pass_x(3)
    send_q(2, 1)
    fresh.pass_x(0)
    fresh.send_x(1)
    fresh.send_x(3)
    send_q(2, 0)
    prefix.pass_x(2)
    fresh.send_x(2)
    send_q(3, 1)
    for d in (1, 3, 2):
        fresh.pass_x(d)
    q_right[3, 0].wait_recv()
    q_left[3, 1].wait_recv()
    q_right[4, 1].wait_recv()
    q_left[4, 0].wait_recv()
    for rows in (prefix, fresh):
        for copy in rows.far.values():
            copy.wait_recv()

    old_keys, new_keys = XN * YN * PRE, XN * YN * NEW
    for h in range(KV):
        vt[h, 0:HD, 0:old_keys] = kvp[KV + h].reshape(old_keys, HD).T
        vt[h, 0:HD, old_keys:] = kvn[KV + h].reshape(new_keys, HD).T

    tile = 256
    old_tiles, new_tiles = old_keys // tile, new_keys // tile

    def attend(slot, h, scores):
        queries = qbuf[slot, h]
        top = jnp.full((8, QN), -jnp.inf, F32)
        for k in range(old_tiles + new_tiles):
            if k < old_tiles:
                keys = kvp[h, k].reshape(tile, HD)
                s = lax.dot_general(keys, queries, NT, preferred_element_type=F32)
            else:
                n = k - old_tiles
                keys = kvn[h, pl.ds(2 * n, 2)].reshape(tile, HD)
                s = lax.dot_general(keys, queries, NT, preferred_element_type=F32)
                s = s + bias[n * tile : (n + 1) * tile, :]
            scores[k * tile : (k + 1) * tile, :] = s
            top = jnp.maximum(top, jnp.max(s.reshape(tile // 8, 8, QN), axis=0))
        top = jnp.max(top, axis=0, keepdims=True) * LOG_SCALE
        top = top.astype(BF16).astype(F32)
        total = jnp.zeros((MSG, QN), F32)
        for k in range(old_tiles + new_tiles):
            p = jnp.exp2(scores[k * tile : (k + 1) * tile, :] * LOG_SCALE - top).astype(BF16)
            total = total + jnp.dot(
                vt[h, :, k * tile : (k + 1) * tile], p, preferred_element_type=F32
            )
        return total[0:HD], total[HD : HD + 1], top

    def merged(mine, message):
        weighted, row_sum, top = mine
        tail = message[HD:MSG, :].astype(F32)
        other_top, other_sum = tail[0:1], tail[1:2] + tail[2:3]
        both = jnp.maximum(top, other_top)
        here, there = jnp.exp2(top - both), jnp.exp2(other_top - both)
        weighted = weighted * here + message[0:HD, :].astype(F32) * there
        return weighted, row_sum * here + other_sum * there, both

    tail_row = lax.broadcasted_iota(jnp.int32, (TAIL, QN), 0)

    def store(ref, state):
        weighted, row_sum, top = state
        ref[0:HD, :] = weighted.astype(BF16)
        high = row_sum.astype(BF16).astype(F32)
        tail = jnp.where(tail_row == 0, top, jnp.where(tail_row == 1, high, row_sum - high))
        ref[HD:MSG, :] = tail.astype(BF16)

    ring = used[0]

    def message(side, step):
        index = ring + side * 7 + step
        return pltpu.make_async_remote_copy(
            src_ref=sent.at[side, step], dst_ref=landed.at[side, step + 2],
            send_sem=send_sem.at[index], recv_sem=recv_sem.at[index],
            device_id=at_z(1 - 2 * side), device_id_type=MESH,
        )

    def advance(step, carry):
        place = (step + 1) // 2
        from_left = jnp.where(place == 0, FAR, 4 - place)
        from_right = jnp.where(place == 0, FAR, 7 - place)
        h = step % 2
        mine_right = attend(from_right, 1 - h, scores_r)
        mine_left = attend(from_left, h, scores_l)

        @pl.when(step >= 2)
        def _():
            message(0, step - 2).wait_recv()
            message(1, step - 2).wait_recv()

        store(sent.at[0, step], merged(mine_right, landed.at[0, step]))
        message(0, step).start()
        store(sent.at[1, step], merged(mine_left, landed.at[1, step]))
        message(1, step).start()
        return carry

    lax.fori_loop(0, 7, advance, 0)

    own = [attend(0, 0, scores_r), attend(0, 1, scores_l)]
    for side in range(2):
        for step in (5, 6):
            message(side, step).wait_recv()
    for h in range(KV):
        state = merged(own[h], landed.at[0, 7 + h])
        weighted, row_sum, _ = merged(state, landed.at[1, 8 - h])
        wide[pl.ds(h, QN, stride=2), :] = (weighted / row_sum).T
    out_ref[...] = wide[0 : KV * QN, :].astype(BF16)

    for copy in started:
        copy.wait_send()

    def finish(step, carry):
        message(0, step).wait_send()
        message(1, step).wait_send()
        return carry

    lax.fori_loop(0, 7, finish, 0)


def on_device(
    queries, features, adapter_down, adapter_key_up, adapter_value_up,
    base_key, base_value, prefix_key, prefix_value, adapter_ids, block_order,
):
    copies = 7 + 3 + 14 + 2 * 19 + 14
    all_keys = XN * YN * (PRE + NEW)
    vmem = pl.BlockSpec(memory_space=pltpu.VMEM)
    smem = pl.BlockSpec(memory_space=pltpu.SMEM)
    hbm = pl.BlockSpec(memory_space=pl.ANY)
    result = pl.pallas_call(
        kernel,
        out_shape=jax.ShapeDtypeStruct((KV * QN, HD), BF16),
        in_specs=[smem, smem, vmem, vmem, vmem, vmem, vmem, hbm, hbm, hbm, hbm],
        out_specs=vmem,
        scratch_shapes=[
            pltpu.VMEM((2, KV * PRE, HD), BF16),
            pltpu.VMEM((2, KV * NEW, HD), BF16),
            pltpu.VMEM((KV * QN, HD), F32),
            pltpu.VMEM((2 * KV, 2 * RANK, HD), BF16),
            pltpu.VMEM((2 * KV, NEW, HD), F32),
            pltpu.VMEM((TEAM, 16, HD), F32),
            pltpu.VMEM((TEAM, 16, HD), F32),
            pltpu.VMEM((HEADS, 16, HD), F32),
            pltpu.VMEM((TEAM, KV, QN, HD), BF16),
            pltpu.VMEM((2 * KV, XN, YN, PRE, HD), BF16),
            pltpu.VMEM((2 * KV, XN, YN, NEW, HD), BF16),
            pltpu.VMEM((KV, MSG, all_keys), BF16),
            pltpu.VMEM((XN * YN * NEW, QN), F32),
            pltpu.VMEM((all_keys, QN), F32),
            pltpu.VMEM((all_keys, QN), F32),
            pltpu.VMEM((2, 7, MSG, QN), BF16),
            pltpu.VMEM((2, 9, MSG, QN), BF16),
            pltpu.SemaphoreType.DMA((4,)),
            pltpu.SemaphoreType.DMA((copies,)),
            pltpu.SemaphoreType.DMA((copies,)),
        ],
        compiler_params=pltpu.CompilerParams(
            collective_id=0, has_side_effects=True, vmem_limit_bytes=40 * 1024 * 1024
        ),
    )(
        adapter_ids,
        block_order,
        queries.reshape(KV * QN, HD),
        features,
        jnp.swapaxes(adapter_down, 1, 2),
        adapter_key_up.reshape(-1, RANK * KV, HD),
        adapter_value_up.reshape(-1, RANK * KV, HD),
        base_key.reshape(-1, HD),
        base_value.reshape(-1, HD),
        prefix_key.reshape(-1, HD),
        prefix_value.reshape(-1, HD),
    )
    return result.reshape(QN, KV, 1, HD)


def solution(mesh):
    placed = (
        P("blk", "head", "team", None),
        P("blk", ("team", "head")),
        P(None, ("team", "head"), None),
        P(None, None, "head", None),
        P(None, None, "head", None),
        P("blk", "head", None),
        P("blk", "head", None),
        P("blk", "head", None),
        P("blk", "head", None),
        P(),
        P(),
    )
    return jax.shard_map(
        on_device,
        mesh=mesh,
        in_specs=placed,
        out_specs=P("blk", "head", "team", None),
        check_vma=False,
    )
```

```python
import math

import jax
import jax.numpy as jnp
from jax import lax
from jax.experimental import pallas as pl
from jax.experimental.pallas import tpu as pltpu
from jax.sharding import PartitionSpec as P

MESH = pl.DeviceIdType.MESH
BF16 = jnp.bfloat16
F32 = jnp.float32

TEAM, XN, YN = 8, 4, 4
QN, HD, KV = 256, 128, 2
PRE, NEW = 128, 64
PIECE = 2 * (PRE + NEW)
RANK, ADAPTERS = 64, 4
LOG_SCALE = math.log2(math.e) / math.sqrt(HD)
TAIL = 16
MSG = HD + TAIL
NT = (((1,), (1,)), ((), ()))
DIST = (4, 3, 5, 2, 6, 1, 7, 0)
COLUMNS = (0, 1, -1, 2)
GROUP = 6 * PRE
FIRST = [(0, 0), (1, 0), (2, 0), (3, 0), (0, 1), (0, 3)]
SECOND = [(1, 1), (2, 1), (3, 1), (1, 3), (2, 3), (3, 3)]
LAST = [(0, 2), (1, 2), (2, 2), (3, 2)]


def kernel(
    ids_ref, order_ref, q_hbm, feat_hbm, down_hbm, kup_hbm, vup_hbm, bk_hbm, bv_hbm, pk_hbm, pv_hbm,
    out_ref,
    q_ref, feat_ref, down_ref, up_ref, pre_ref, base_ref, wide, own_rows, ups, lat_part, lat_sib,
    lat_chip, lat_team, lat_pair, lat_all, q_own, qbuf, kv, keys, values, vt, bias, scores_a, scores_b,
    acc, tops, sent, from_sib, landed, local_sem, send_sem, recv_sem, core_send, core_recv, home_send, home_recv,
):
    team = lax.axis_index("team")
    blk = lax.axis_index("blk")
    head = lax.axis_index("head")
    yh, x = blk // XN, blk % XN
    ylo, core = head // 2, head % 2
    half, mine = team // 4, team % 2
    is_owner = (team % 4) // 2 == core
    not_owner = jnp.logical_not(is_owner)

    def at_z(d):
        return {"team": (team + d + TEAM) % TEAM}

    def at_blk(dy, dx):
        return {"blk": ((yh + dy + YN) % YN) * XN + (x + dx + XN) % XN}

    sibling = {"head": ylo * 2 + 1 - core}
    beside = {"head": (1 - ylo) * 2 + core}
    others = [(d, c) for d in range(YN) for c in range(XN) if (d, c) != (0, 0)]

    barrier = pltpu.get_barrier_semaphore()
    peers = [at_z(d) for d in range(1, TEAM)] + [sibling, beside]
    peers += [at_blk(d, COLUMNS[c]) for d, c in others]
    for peer in peers:
        pl.semaphore_signal(barrier, inc=1, device_id=peer, device_id_type=MESH)

    used = [0]

    def link(src, dst, peer):
        index = used[0]
        used[0] += 1
        return pltpu.make_async_remote_copy(
            src_ref=src, dst_ref=dst, send_sem=send_sem.at[index], recv_sem=recv_sem.at[index],
            device_id=peer, device_id_type=MESH,
        )

    pre_rows = pl.ds(pl.multiple_of(half * (KV * 2 * PRE), KV * 2 * PRE), KV * 2 * PRE)
    base_rows = pl.ds(pl.multiple_of(half * (KV * 2 * NEW), KV * 2 * NEW), KV * 2 * NEW)
    pairs = [
        (feat_hbm, feat_ref), (down_hbm, down_ref), (q_hbm, q_ref),
        (pk_hbm.at[pre_rows], pre_ref.at[0]), (pv_hbm.at[pre_rows], pre_ref.at[1]),
        (bk_hbm.at[base_rows], base_ref.at[0]), (bv_hbm.at[base_rows], base_ref.at[1]),
        (kup_hbm, up_ref.at[0]), (vup_hbm, up_ref.at[1]),
    ]
    local = [pltpu.make_async_copy(src, dst, local_sem.at[k]) for k, (src, dst) in enumerate(pairs)]
    for copy in local:
        copy.start()

    for copy in local[:2]:
        copy.wait()
    down = down_ref[ids_ref[blk]]
    partial = lax.dot_general(
        feat_ref[...], jnp.concatenate([down, down], axis=0), NT, preferred_element_type=F32
    )
    first_half = lax.broadcasted_iota(jnp.int32, (32, HD), 1) < RANK
    for quarter in range(4):
        row = quarter * NEW
        lat_part[quarter % 2, quarter // 2] = jnp.where(
            first_half, partial[row : row + 32], partial[row + 32 : row + 64]
        )

    for copy in local[2:]:
        copy.wait()
    wide[0 : KV * QN, :] = q_ref[...].astype(F32)
    for h in range(KV):
        q_own[h] = wide[pl.ds(h, QN, stride=2), :].astype(BF16)

    @pl.when(is_owner)
    def _():
        def pick(rows, count):
            wide[0 : 2 * count, :] = rows.astype(F32)
            even, odd = (wide[pl.ds(h, count, stride=2), :] for h in range(KV))
            return jnp.where(mine == 0, even, odd).astype(BF16)

        for kind in range(2):
            rows = pick(pre_ref[kind], 2 * PRE)
            fresh = pick(base_ref[kind], 2 * NEW)
            for c in range(2):
                own_rows[c, kind * PRE : (kind + 1) * PRE, :] = rows[c * PRE : (c + 1) * PRE]
                at = 2 * PRE + kind * NEW
                own_rows[c, at : at + NEW, :] = fresh[c * NEW : (c + 1) * NEW]
            for a in range(ADAPTERS):
                ups[a, :, kind * HD : (kind + 1) * HD] = pick(up_ref[kind, a], RANK)
        kv[0, 0] = own_rows[core]
        qbuf[7] = q_own[mine]

    pl.semaphore_wait(barrier, len(peers))

    lat_core = link(lat_part.at[1 - core], lat_sib, sibling)
    share_rows = link(own_rows.at[1 - core], kv.at[0, 0], sibling)
    share_ups = link(ups, ups, sibling)
    share_q = [link(qbuf.at[i], qbuf.at[i], sibling) for i in range(TEAM)]
    team_q = [
        link(q_own.at[(team + DIST[i]) % 2], qbuf.at[i], at_z(DIST[i])) for i in range(TEAM - 1)
    ]
    takes_q = [((team + DIST[i]) % 4) // 2 == core for i in range(TEAM - 1)]

    lat_core.start()

    @pl.when(is_owner)
    def _():
        share_rows.start()

    lat_core.wait_recv()
    for h in range(2):
        lat_chip[h] = lat_part[core, h] + lat_sib[h]
    lat_z = [
        link(lat_chip.at[((team + d) % TEAM) // 4], lat_team.at[d], at_z(d)) for d in range(1, TEAM)
    ]
    for copy in lat_z:
        copy.start()
    for i in range(TEAM - 1):
        pl.when(takes_q[i])(team_q[i].start)

    @pl.when(not_owner)
    def _():
        share_rows.wait_recv()

    down_y = {d: link(kv.at[0, 0], kv.at[0, d], at_blk(d, 0)) for d in (1, 3, 2)}
    round_x = {}

    def send_x(d):
        if d:
            down_y[d].wait_recv()
        for c in (1, 2, 3):
            round_x[c, d] = link(kv.at[0, d], kv.at[c, d], at_blk(0, COLUMNS[c]))
            round_x[c, d].start()

    for copy in down_y.values():
        copy.start()
    send_x(0)

    @pl.when(is_owner)
    def _():
        share_ups.start()
        share_q[7].start()

    token = order_ref[blk] * QN + lax.broadcasted_iota(jnp.int32, (NEW, QN), 1)
    within = (2 * half + core) * NEW + lax.broadcasted_iota(jnp.int32, (NEW, QN), 0)

    def owner_of(column, d):
        return ((yh - d + YN) % YN) * XN + (x - COLUMNS[column] + XN) % XN

    for k, (column, d) in enumerate(FIRST + SECOND + LAST):
        hidden = order_ref[owner_of(column, d)] * QN + within > token
        bias[k * NEW : (k + 1) * NEW, :] = jnp.where(hidden, -1e30, 0.0)
    for group in range(4):
        vt[group, HD:MSG, :] = jnp.ones((TAIL, GROUP), BF16)

    send_x(1)
    send_x(3)

    for copy in lat_z:
        copy.wait_recv()
    total = lat_chip[half]
    for d in range(1, TEAM):
        total = total + lat_team[d]
    lat_pair[0] = total
    lat_y = link(lat_pair.at[0], lat_pair.at[1], beside)
    lat_y.start()

    @pl.when(is_owner)
    def _():
        for i in (5, 6, 3, 4, 1, 2, 0):
            team_q[i].wait_recv()
            share_q[i].start()

    lat_y.wait_recv()
    lat_all[0, 0] = (lat_pair[0] + lat_pair[1]).astype(BF16)
    lat_blk = {
        (c, d): link(lat_all.at[0, 0], lat_all.at[c, d], at_blk(d, COLUMNS[c])) for d, c in others
    }
    for copy in lat_blk.values():
        copy.start()

    send_x(2)

    @pl.when(not_owner)
    def _():
        for i in range(TEAM):
            share_q[i].wait_recv()
        share_ups.wait_recv()

    def put_prefix(group, at, slot):
        keys[group, at : at + PRE, :] = kv[slot[0], slot[1], 0:PRE, :]
        values[group, at : at + PRE, :] = kv[slot[0], slot[1], PRE : 2 * PRE, :]

    def put_fresh(group, at, slot):
        packed = lat_all[slot[0], slot[1]].astype(F32)
        latent = jnp.concatenate(
            [jnp.where(first_half, packed, 0.0), jnp.where(first_half, 0.0, packed)], axis=0
        ).astype(BF16)
        up = ups[ids_ref[owner_of(*slot)]]
        delta = jnp.dot(latent, jnp.concatenate([up, up], axis=0), preferred_element_type=F32)
        base = kv[slot[0], slot[1], 2 * PRE : PIECE, :].astype(F32)
        keys[group, at : at + NEW, :] = (base[0:NEW] + delta[:, 0:HD]).astype(BF16)
        values[group, at : at + NEW, :] = (base[NEW:] + delta[:, HD:]).astype(BF16)

    def turn(group):
        vt[group, 0:HD, :] = values[group].T

    def step(group, i, scores):
        s = lax.dot_general(keys[group], qbuf[i], NT, preferred_element_type=F32)
        if group == 2:
            s = s + bias[0:GROUP, :]
        if group == 3:
            plain = 4 * PRE
            s = jnp.concatenate([s[0:plain], s[plain:] + bias[GROUP:, :]], axis=0)
        scores[...] = s
        top = jnp.max(s.reshape(GROUP // 8, 8, QN), axis=0)
        top = jnp.max(top, axis=0, keepdims=True) * LOG_SCALE
        top = top.astype(BF16).astype(F32)
        if group:
            before = tops[i, 0:1, :]
            top = jnp.maximum(top, before)
        p = jnp.exp2(scores[...] * LOG_SCALE - top).astype(BF16)
        weighted = jnp.dot(vt[group], p, preferred_element_type=F32)
        if group:
            weighted = weighted + acc[i] * jnp.exp2(before - top)
        acc[i] = weighted
        tops[i] = jnp.broadcast_to(top, (8, QN))

    def run(group):
        def both(k, carry):
            step(group, 2 * k, scores_a)
            step(group, 2 * k + 1, scores_b)
            return carry

        lax.fori_loop(0, TEAM // 2, both, 0)

    for k, slot in enumerate(FIRST):
        if slot[0]:
            round_x[slot].wait_recv()
        put_prefix(0, k * PRE, slot)
    turn(0)
    run(0)

    for k, slot in enumerate(SECOND):
        round_x[slot].wait_recv()
        put_prefix(1, k * PRE, slot)
    turn(1)
    run(1)

    for copy in lat_blk.values():
        copy.wait_recv()
    for k, slot in enumerate(FIRST + SECOND):
        put_fresh(2, k * NEW, slot)
    turn(2)
    run(2)

    for k, slot in enumerate(LAST):
        if slot[0]:
            round_x[slot].wait_recv()
        put_prefix(3, k * PRE, slot)
        put_fresh(3, 4 * PRE + k * NEW, slot)
    turn(3)

    tail_row = lax.broadcasted_iota(jnp.int32, (TAIL, QN), 0)

    def store(ref, state):
        weighted, row_sum, top = state
        ref[0:HD, :] = weighted.astype(BF16)
        high = row_sum.astype(BF16).astype(F32)
        tail = jnp.where(tail_row == 0, top, jnp.where(tail_row == 1, high, row_sum - high))
        ref[HD:MSG, :] = tail.astype(BF16)

    def held(i):
        return acc[i, 0:HD, :], acc[i, HD : HD + 1, :], tops[i, 0:1, :]

    def read(ref):
        tail = ref[HD:MSG, :].astype(F32)
        return ref[0:HD, :].astype(F32), tail[1:2] + tail[2:3], tail[0:1]

    def merged(one, other):
        top = jnp.maximum(one[2], other[2])
        a, b = jnp.exp2(one[2] - top), jnp.exp2(other[2] - top)
        return one[0] * a + other[0] * b, one[1] * a + other[1] * b, top

    home_slot = mine * 2 + half

    def to_sibling(i):
        return pltpu.make_async_remote_copy(
            src_ref=sent.at[i], dst_ref=from_sib.at[i], send_sem=core_send.at[i], recv_sem=core_recv.at[i],
            device_id=sibling, device_id_type=MESH,
        )

    def homeward(i, slot):
        away = jnp.where(i % 2 == 0, 4 + i // 2, 4 - (i + 1) // 2)
        return pltpu.make_async_remote_copy(
            src_ref=sent.at[i], dst_ref=landed.at[slot], send_sem=home_send.at[i], recv_sem=home_recv.at[slot],
            device_id={"team": (team - away + TEAM) % TEAM}, device_id_type=MESH,
        )

    def merge_and_send(i):
        to_sibling(i).wait_recv()
        store(sent.at[i], merged(held(i), read(from_sib.at[i])))
        homeward(i, home_slot).start()

    def final(k, carry):
        step(3, 2 * k, scores_a)
        step(3, 2 * k + 1, scores_b)

        @pl.when(not_owner)
        def _():
            for i in (2 * k, 2 * k + 1):
                store(sent.at[i], held(i))
                to_sibling(i).start()

        @pl.when(jnp.logical_and(is_owner, k > 0))
        def _():
            for i in (2 * k - 2, 2 * k - 1):
                merge_and_send(i)

        return carry

    lax.fori_loop(0, TEAM // 2, final, 0)

    @pl.when(is_owner)
    def _():
        merge_and_send(6)
        to_sibling(7).wait_recv()
        store(landed.at[home_slot], merged(held(7), read(from_sib.at[7])))

    for h in range(KV):
        for part in range(2):
            slot = h * 2 + part

            @pl.when(team != part * 4 + core * 2 + h)
            def _():
                homeward(0, slot).wait_recv()

        weighted, row_sum, _ = merged(read(landed.at[h * 2]), read(landed.at[h * 2 + 1]))
        wide[pl.ds(h, QN, stride=2), :] = (weighted / row_sum).T
    out_ref[...] = wide[0 : KV * QN, :].astype(BF16)

    for copy in [lat_core, lat_y, *lat_z, *down_y.values(), *round_x.values(), *lat_blk.values()]:
        copy.wait_send()
    for i in range(TEAM - 1):
        pl.when(takes_q[i])(team_q[i].wait_send)

    @pl.when(is_owner)
    def _():
        for copy in [share_rows, share_ups, *share_q]:
            copy.wait_send()

        def gone(i, carry):
            homeward(i, home_slot).wait_send()
            return carry

        lax.fori_loop(0, TEAM - 1, gone, 0)

    @pl.when(not_owner)
    def _():
        def gone(i, carry):
            to_sibling(i).wait_send()
            return carry

        lax.fori_loop(0, TEAM, gone, 0)


def on_device(
    queries, features, adapter_down, adapter_key_up, adapter_value_up,
    base_key, base_value, prefix_key, prefix_value, adapter_ids, block_order,
):
    copies = 1 + 1 + 1 + 8 + 7 + 7 + 1 + 15 + 3 + 12
    vmem = pl.BlockSpec(memory_space=pltpu.VMEM)
    smem = pl.BlockSpec(memory_space=pltpu.SMEM)
    hbm = pl.BlockSpec(memory_space=pl.ANY)
    dma = pltpu.SemaphoreType.DMA
    result = pl.pallas_call(
        kernel,
        out_shape=jax.ShapeDtypeStruct((KV * QN, HD), BF16),
        in_specs=[smem] * 2 + [hbm] * 9,
        out_specs=vmem,
        scratch_shapes=[
            pltpu.VMEM((KV * QN, HD), BF16),
            pltpu.VMEM(features.shape, BF16),
            pltpu.VMEM((ADAPTERS, RANK, features.shape[1]), BF16),
            pltpu.VMEM((2, ADAPTERS, KV * RANK, HD), BF16),
            pltpu.VMEM((2, KV * 2 * PRE, HD), BF16),
            pltpu.VMEM((2, KV * 2 * NEW, HD), BF16),
            pltpu.VMEM((KV * QN, HD), F32),
            pltpu.VMEM((2, PIECE, HD), BF16),
            pltpu.VMEM((ADAPTERS, RANK, 2 * HD), BF16),
            pltpu.VMEM((2, 2, 32, HD), F32),
            pltpu.VMEM((2, 32, HD), F32),
            pltpu.VMEM((2, 32, HD), F32),
            pltpu.VMEM((TEAM, 32, HD), F32),
            pltpu.VMEM((2, 32, HD), F32),
            pltpu.VMEM((XN, YN, 32, HD), BF16),
            pltpu.VMEM((KV, QN, HD), BF16),
            pltpu.VMEM((TEAM, QN, HD), BF16),
            pltpu.VMEM((XN, YN, PIECE, HD), BF16),
            pltpu.VMEM((4, GROUP, HD), BF16),
            pltpu.VMEM((4, GROUP, HD), BF16),
            pltpu.VMEM((4, MSG, GROUP), BF16),
            pltpu.VMEM((XN * YN * NEW, QN), F32),
            pltpu.VMEM((GROUP, QN), F32),
            pltpu.VMEM((GROUP, QN), F32),
            pltpu.VMEM((TEAM, MSG, QN), F32),
            pltpu.VMEM((TEAM, 8, QN), F32),
            pltpu.VMEM((TEAM, MSG, QN), BF16),
            pltpu.VMEM((TEAM, MSG, QN), BF16),
            pltpu.VMEM((4, MSG, QN), BF16),
            dma((9,)),
            dma((copies,)),
            dma((copies,)),
            dma((TEAM,)),
            dma((TEAM,)),
            dma((TEAM,)),
            dma((4,)),
        ],
        compiler_params=pltpu.CompilerParams(
            collective_id=0, has_side_effects=True, vmem_limit_bytes=60 * 1024 * 1024
        ),
    )(
        adapter_ids,
        block_order,
        queries.reshape(KV * QN, HD),
        features,
        jnp.swapaxes(adapter_down, 1, 2),
        adapter_key_up.reshape(-1, RANK * KV, HD),
        adapter_value_up.reshape(-1, RANK * KV, HD),
        base_key.reshape(-1, HD),
        base_value.reshape(-1, HD),
        prefix_key.reshape(-1, HD),
        prefix_value.reshape(-1, HD),
    )
    return result.reshape(QN, KV, 1, HD)


def solution(mesh):
    placed = (
        P("blk", "head", "team", None),
        P("blk", ("team", "head")),
        P(None, ("team", "head"), None),
        P(None, None, "head", None),
        P(None, None, "head", None),
        P("blk", "head", None),
        P("blk", "head", None),
        P("blk", "head", None),
        P("blk", "head", None),
        P(),
        P(),
    )
    return jax.shard_map(
        on_device,
        mesh=mesh,
        in_specs=placed,
        out_specs=P("blk", "head", "team", None),
        check_vma=False,
    )
```

```python
import math

import jax
import jax.numpy as jnp
from jax import lax
from jax.experimental import pallas as pl
from jax.experimental.pallas import tpu as pltpu
from jax.sharding import PartitionSpec as P

MESH = pl.DeviceIdType.MESH
BF16 = jnp.bfloat16
F32 = jnp.float32

TEAM, XN, YN = 8, 4, 4
QN, HD, KV = 256, 128, 2
PRE, NEW = 128, 64
PIECE = 2 * (PRE + NEW)
RANK, ADAPTERS = 64, 4
LOG_SCALE = math.log2(math.e) / math.sqrt(HD)
TAIL = 16
MSG = HD + TAIL
NT = (((1,), (1,)), ((), ()))
DIST = (4, 3, 5, 2, 6, 1, 7, 0)
COLUMNS = (0, 1, -1, 2)
FIRST = [(0, 0), (1, 0), (2, 0), (3, 0), (0, 1), (0, 3), (0, 2)]
SECOND = [(1, 1), (2, 1), (3, 1), (1, 3), (2, 3), (3, 3)]
LAST = [(1, 2), (2, 2), (3, 2)]
ALL = FIRST + SECOND + LAST
SIZES = (len(FIRST) * PRE, len(SECOND) * PRE, len(ALL) * NEW, len(LAST) * PRE)
STARTS = tuple(sum(SIZES[:k]) for k in range(4))
FRESH = 2
KEYS = sum(SIZES)
KEY_AT, VALUE_AT = 2 * NEW, 2 * NEW + PRE
HALVES = (pl.ds(0, PIECE // 2), pl.ds(PIECE // 2, PIECE // 2))


def kernel(
    ids_ref, order_ref, q_hbm, feat_hbm, down_hbm, kup_hbm, vup_hbm, bk_hbm, bv_hbm, pk_hbm, pv_hbm,
    out_ref,
    q_ref, feat_ref, down_ref, up_ref, pre_ref, base_ref, wide, own_rows, ups, lat_part, lat_sib,
    lat_chip, lat_team, lat_pair, lat_all, q_own, qbuf, kv, keys, values, vt, bias, scores,
    acc, tops, sent, from_sib, landed, local_sem, send_sem, recv_sem, core_send, core_recv, home_send, home_recv,
):
    team = lax.axis_index("team")
    blk = lax.axis_index("blk")
    head = lax.axis_index("head")
    yh, x = blk // XN, blk % XN
    ylo, core = head // 2, head % 2
    half, mine = team // 4, team % 2
    is_owner = (team % 4) // 2 == core
    not_owner = jnp.logical_not(is_owner)

    def at_z(d):
        return {"team": (team + d + TEAM) % TEAM}

    def at_blk(dy, dx):
        return {"blk": ((yh + dy + YN) % YN) * XN + (x + dx + XN) % XN}

    sibling = {"head": ylo * 2 + 1 - core}
    beside = {"head": (1 - ylo) * 2 + core}
    others = [(d, c) for d in range(YN) for c in range(XN) if (d, c) != (0, 0)]

    barrier = pltpu.get_barrier_semaphore()
    peers = [at_z(d) for d in range(1, TEAM)] + [sibling, beside]
    peers += [at_blk(d, COLUMNS[c]) for d, c in others]
    for peer in peers:
        pl.semaphore_signal(barrier, inc=1, device_id=peer, device_id_type=MESH)

    used = [0]

    def link(src, dst, peer):
        index = used[0]
        used[0] += 1
        return pltpu.make_async_remote_copy(
            src_ref=src, dst_ref=dst, send_sem=send_sem.at[index], recv_sem=recv_sem.at[index],
            device_id=peer, device_id_type=MESH,
        )

    pre_rows = pl.ds(pl.multiple_of(half * (KV * 2 * PRE), KV * 2 * PRE), KV * 2 * PRE)
    base_rows = pl.ds(pl.multiple_of(half * (KV * 2 * NEW), KV * 2 * NEW), KV * 2 * NEW)
    pairs = [
        (feat_hbm, feat_ref), (down_hbm, down_ref), (q_hbm, q_ref),
        (pk_hbm.at[pre_rows], pre_ref.at[0]), (pv_hbm.at[pre_rows], pre_ref.at[1]),
        (bk_hbm.at[base_rows], base_ref.at[0]), (bv_hbm.at[base_rows], base_ref.at[1]),
        (kup_hbm, up_ref.at[0]), (vup_hbm, up_ref.at[1]),
    ]
    local = [pltpu.make_async_copy(src, dst, local_sem.at[k]) for k, (src, dst) in enumerate(pairs)]
    for copy in local:
        copy.start()

    for copy in local[:2]:
        copy.wait()
    down = down_ref[ids_ref[blk]]
    partial = lax.dot_general(
        feat_ref[...], jnp.concatenate([down, down], axis=0), NT, preferred_element_type=F32
    )
    first_half = lax.broadcasted_iota(jnp.int32, (32, HD), 1) < RANK
    for quarter in range(4):
        row = quarter * NEW
        lat_part[quarter % 2, quarter // 2] = jnp.where(
            first_half, partial[row : row + 32], partial[row + 32 : row + 64]
        )

    for copy in local[2:]:
        copy.wait()
    wide[0 : KV * QN, :] = q_ref[...].astype(F32)
    for h in range(KV):
        q_own[h] = wide[pl.ds(h, QN, stride=2), :].astype(BF16)

    @pl.when(is_owner)
    def _():
        def pick(rows, count):
            wide[0 : 2 * count, :] = rows.astype(F32)
            even, odd = (wide[pl.ds(h, count, stride=2), :] for h in range(KV))
            return jnp.where(mine == 0, even, odd).astype(BF16)

        for kind in range(2):
            rows = pick(pre_ref[kind], 2 * PRE)
            fresh = pick(base_ref[kind], 2 * NEW)
            for c in range(2):
                at = KEY_AT + kind * PRE
                own_rows[c, at : at + PRE, :] = rows[c * PRE : (c + 1) * PRE]
                own_rows[c, kind * NEW : (kind + 1) * NEW, :] = fresh[c * NEW : (c + 1) * NEW]
            for a in range(ADAPTERS):
                ups[a, :, kind * HD : (kind + 1) * HD] = pick(up_ref[kind, a], RANK)
        kv[0, 0] = own_rows[core]
        qbuf[3, QN:, :] = q_own[mine]

    pl.semaphore_wait(barrier, len(peers))

    def q_slot(i):
        return qbuf.at[i // 2, pl.ds((i % 2) * QN, QN)]

    lat_core = link(lat_part.at[1 - core], lat_sib, sibling)
    share_rows = link(own_rows.at[1 - core], kv.at[0, 0], sibling)
    share_ups = link(ups, ups, sibling)
    share_q = [link(q_slot(i), q_slot(i), sibling) for i in range(TEAM)]
    team_q = [
        link(q_own.at[(team + DIST[i]) % 2], q_slot(i), at_z(DIST[i])) for i in range(TEAM - 1)
    ]
    takes_q = [((team + DIST[i]) % 4) // 2 == core for i in range(TEAM - 1)]

    down_y = {
        (d, h): link(kv.at[0, 0, HALVES[h]], kv.at[0, d, HALVES[h]], at_blk(d, 0))
        for d, h in ((1, 0), (3, 0), (1, 1), (3, 1), (2, 0), (2, 1))
    }
    round_x = {}

    def send_x(d, h):
        if d:
            down_y[d, h].wait_recv()
        for c in (1, 2, 3):
            round_x[c, d, h] = link(kv.at[0, d, HALVES[h]], kv.at[c, d, HALVES[h]], at_blk(0, COLUMNS[c]))
            round_x[c, d, h].start()

    @pl.when(is_owner)
    def _():
        share_rows.start()

    lat_core.start()

    @pl.when(not_owner)
    def _():
        share_rows.wait_recv()

    for copy in down_y.values():
        copy.start()
    send_x(0, 0)
    send_x(0, 1)

    lat_core.wait_recv()
    for h in range(2):
        lat_chip[h] = lat_part[core, h] + lat_sib[h]
    lat_z = [
        link(lat_chip.at[((team + d) % TEAM) // 4], lat_team.at[d], at_z(d)) for d in range(1, TEAM)
    ]
    for copy in lat_z:
        copy.start()
    for i in range(TEAM - 1):
        pl.when(takes_q[i])(team_q[i].start)

    @pl.when(is_owner)
    def _():
        share_ups.start()
        share_q[7].start()

    token = order_ref[blk] * QN + lax.broadcasted_iota(jnp.int32, (NEW, QN), 1)
    within = (2 * half + core) * NEW + lax.broadcasted_iota(jnp.int32, (NEW, QN), 0)

    def owner_of(column, d):
        return ((yh - d + YN) % YN) * XN + (x - COLUMNS[column] + XN) % XN

    for k, (column, d) in enumerate(ALL):
        hidden = order_ref[owner_of(column, d)] * QN + within > token
        bias[k * NEW : (k + 1) * NEW, :] = jnp.where(hidden, -1e30, 0.0)
    vt[HD:MSG, :] = jnp.ones((TAIL, KEYS), BF16)

    send_x(1, 0)
    send_x(3, 0)
    send_x(1, 1)
    send_x(3, 1)

    for copy in lat_z:
        copy.wait_recv()
    total = lat_chip[half]
    for d in range(1, TEAM):
        total = total + lat_team[d]
    lat_pair[0] = total
    lat_y = link(lat_pair.at[0], lat_pair.at[1], beside)
    lat_y.start()

    @pl.when(is_owner)
    def _():
        for i in (5, 6, 3, 4, 1, 2, 0):
            team_q[i].wait_recv()
            share_q[i].start()

    lat_y.wait_recv()
    lat_all[0, 0] = (lat_pair[0] + lat_pair[1]).astype(BF16)
    lat_blk = {
        (c, d): link(lat_all.at[0, 0], lat_all.at[c, d], at_blk(d, COLUMNS[c])) for d, c in others
    }
    for copy in lat_blk.values():
        copy.start()

    send_x(2, 0)
    send_x(2, 1)

    @pl.when(not_owner)
    def _():
        for i in range(TEAM):
            share_q[i].wait_recv()
        share_ups.wait_recv()

    def arrived(slot, h):
        if slot[0]:
            round_x[slot[0], slot[1], h].wait_recv()

    def put_prefix(at, slot):
        keys[at : at + PRE, :] = kv[slot[0], slot[1], KEY_AT:VALUE_AT, :]
        values[at : at + PRE, :] = kv[slot[0], slot[1], VALUE_AT:PIECE, :]

    def put_fresh(at, slot):
        packed = lat_all[slot[0], slot[1]].astype(F32)
        latent = jnp.concatenate(
            [jnp.where(first_half, packed, 0.0), jnp.where(first_half, 0.0, packed)], axis=0
        ).astype(BF16)
        up = ups[ids_ref[owner_of(*slot)]]
        delta = jnp.dot(latent, jnp.concatenate([up, up], axis=0), preferred_element_type=F32)
        base = kv[slot[0], slot[1], 0 : 2 * NEW, :].astype(F32)
        keys[at : at + NEW, :] = (base[0:NEW] + delta[:, 0:HD]).astype(BF16)
        values[at : at + NEW, :] = (base[NEW:] + delta[:, HD:]).astype(BF16)

    def turn(group):
        at, size = STARTS[group], SIZES[group]
        vt[0:HD, at : at + size] = values[at : at + size, :].T

    def score(group, k):
        at, size = STARTS[group], SIZES[group]
        s = lax.dot_general(keys[at : at + size, :], qbuf[k], NT, preferred_element_type=F32)
        if group == FRESH:
            s = s + jnp.concatenate([bias[...], bias[...]], axis=1)
        scores[k % 2, 0:size, :] = s
        top = jnp.max(s.reshape(size // 8, 8, 2 * QN), axis=0)
        top = jnp.max(top, axis=0, keepdims=True) * LOG_SCALE
        return top.astype(BF16).astype(F32)

    def weigh(group, k, top):
        at, size = STARTS[group], SIZES[group]
        if group:
            before = tops[k, 0:1, :]
            top = jnp.maximum(top, before)
        p = jnp.exp2(scores[k % 2, 0:size, :] * LOG_SCALE - top).astype(BF16)
        weighted = jnp.dot(vt[:, at : at + size], p, preferred_element_type=F32)
        if group:
            weighted = weighted + acc[k] * jnp.exp2(before - top)
        acc[k] = weighted
        tops[k] = jnp.broadcast_to(top, (8, 2 * QN))

    def run(group, first=0, count=TEAM // 2):
        top = score(group, first)
        for k in range(first, first + count):
            ahead = score(group, k + 1) if k + 1 < first + count else None
            weigh(group, k, top)
            top = ahead

    for k, slot in enumerate(FIRST):
        for h in range(2):
            arrived(slot, h)
        put_prefix(STARTS[0] + k * PRE, slot)
    turn(0)
    run(0)

    for k, slot in enumerate(SECOND):
        for h in range(2):
            arrived(slot, h)
        put_prefix(STARTS[1] + k * PRE, slot)
    turn(1)
    run(1)

    for copy in lat_blk.values():
        copy.wait_recv()
    for slot in LAST:
        arrived(slot, 0)
    for k, slot in enumerate(ALL):
        put_fresh(STARTS[FRESH] + k * NEW, slot)
    turn(FRESH)
    run(FRESH)

    for k, slot in enumerate(LAST):
        arrived(slot, 1)
        put_prefix(STARTS[3] + k * PRE, slot)
    turn(3)

    tail_row = lax.broadcasted_iota(jnp.int32, (TAIL, QN), 0)

    def store(ref, state):
        weighted, row_sum, top = state
        ref[0:HD, :] = weighted.astype(BF16)
        high = row_sum.astype(BF16).astype(F32)
        tail = jnp.where(tail_row == 0, top, jnp.where(tail_row == 1, high, row_sum - high))
        ref[HD:MSG, :] = tail.astype(BF16)

    def held(i):
        side = slice((i % 2) * QN, (i % 2 + 1) * QN)
        return acc[i // 2, 0:HD, side], acc[i // 2, HD : HD + 1, side], tops[i // 2, 0:1, side]

    def read(ref):
        tail = ref[HD:MSG, :].astype(F32)
        return ref[0:HD, :].astype(F32), tail[1:2] + tail[2:3], tail[0:1]

    def merged(one, other):
        top = jnp.maximum(one[2], other[2])
        a, b = jnp.exp2(one[2] - top), jnp.exp2(other[2] - top)
        return one[0] * a + other[0] * b, one[1] * a + other[1] * b, top

    home_slot = mine * 2 + half

    def to_sibling(i):
        return pltpu.make_async_remote_copy(
            src_ref=sent.at[i], dst_ref=from_sib.at[i], send_sem=core_send.at[i], recv_sem=core_recv.at[i],
            device_id=sibling, device_id_type=MESH,
        )

    def homeward(i, slot):
        away = jnp.where(i % 2 == 0, 4 + i // 2, 4 - (i + 1) // 2)
        return pltpu.make_async_remote_copy(
            src_ref=sent.at[i], dst_ref=landed.at[slot], send_sem=home_send.at[i], recv_sem=home_recv.at[slot],
            device_id={"team": (team - away + TEAM) % TEAM}, device_id_type=MESH,
        )

    def merge_and_send(i):
        to_sibling(i).wait_recv()
        store(sent.at[i], merged(held(i), read(from_sib.at[i])))
        homeward(i, home_slot).start()

    for stage in range(2):
        run(3, 2 * stage, 2)

        @pl.when(not_owner)
        def _():
            for i in range(4 * stage, 4 * stage + 4):
                store(sent.at[i], held(i))
                to_sibling(i).start()

        if stage:

            @pl.when(is_owner)
            def _():
                for i in range(TEAM - 1):
                    merge_and_send(i)
                to_sibling(7).wait_recv()
                store(landed.at[home_slot], merged(held(7), read(from_sib.at[7])))

    for h in range(KV):
        for part in range(2):
            slot = h * 2 + part

            @pl.when(team != part * 4 + core * 2 + h)
            def _():
                homeward(0, slot).wait_recv()

        weighted, row_sum, _ = merged(read(landed.at[h * 2]), read(landed.at[h * 2 + 1]))
        wide[pl.ds(h, QN, stride=2), :] = (weighted / row_sum).T
    out_ref[...] = wide[0 : KV * QN, :].astype(BF16)

    for copy in [lat_core, lat_y, *lat_z, *down_y.values(), *round_x.values(), *lat_blk.values()]:
        copy.wait_send()
    for i in range(TEAM - 1):
        pl.when(takes_q[i])(team_q[i].wait_send)

    @pl.when(is_owner)
    def _():
        for copy in [share_rows, share_ups, *share_q]:
            copy.wait_send()

        def gone(i, carry):
            homeward(i, home_slot).wait_send()
            return carry

        lax.fori_loop(0, TEAM - 1, gone, 0)

    @pl.when(not_owner)
    def _():
        def gone(i, carry):
            to_sibling(i).wait_send()
            return carry

        lax.fori_loop(0, TEAM, gone, 0)


def on_device(
    queries, features, adapter_down, adapter_key_up, adapter_value_up,
    base_key, base_value, prefix_key, prefix_value, adapter_ids, block_order,
):
    copies = 1 + 1 + 1 + 8 + 7 + 7 + 1 + 15 + 6 + 24
    vmem = pl.BlockSpec(memory_space=pltpu.VMEM)
    smem = pl.BlockSpec(memory_space=pltpu.SMEM)
    hbm = pl.BlockSpec(memory_space=pl.ANY)
    dma = pltpu.SemaphoreType.DMA
    result = pl.pallas_call(
        kernel,
        out_shape=jax.ShapeDtypeStruct((KV * QN, HD), BF16),
        in_specs=[smem] * 2 + [hbm] * 9,
        out_specs=vmem,
        scratch_shapes=[
            pltpu.VMEM((KV * QN, HD), BF16),
            pltpu.VMEM(features.shape, BF16),
            pltpu.VMEM((ADAPTERS, RANK, features.shape[1]), BF16),
            pltpu.VMEM((2, ADAPTERS, KV * RANK, HD), BF16),
            pltpu.VMEM((2, KV * 2 * PRE, HD), BF16),
            pltpu.VMEM((2, KV * 2 * NEW, HD), BF16),
            pltpu.VMEM((KV * QN, HD), F32),
            pltpu.VMEM((2, PIECE, HD), BF16),
            pltpu.VMEM((ADAPTERS, RANK, 2 * HD), BF16),
            pltpu.VMEM((2, 2, 32, HD), F32),
            pltpu.VMEM((2, 32, HD), F32),
            pltpu.VMEM((2, 32, HD), F32),
            pltpu.VMEM((TEAM, 32, HD), F32),
            pltpu.VMEM((2, 32, HD), F32),
            pltpu.VMEM((XN, YN, 32, HD), BF16),
            pltpu.VMEM((KV, QN, HD), BF16),
            pltpu.VMEM((TEAM // 2, 2 * QN, HD), BF16),
            pltpu.VMEM((XN, YN, PIECE, HD), BF16),
            pltpu.VMEM((KEYS, HD), BF16),
            pltpu.VMEM((KEYS, HD), BF16),
            pltpu.VMEM((MSG, KEYS), BF16),
            pltpu.VMEM((XN * YN * NEW, QN), F32),
            pltpu.VMEM((2, max(SIZES), 2 * QN), F32),
            pltpu.VMEM((TEAM // 2, MSG, 2 * QN), F32),
            pltpu.VMEM((TEAM // 2, 8, 2 * QN), F32),
            pltpu.VMEM((TEAM, MSG, QN), BF16),
            pltpu.VMEM((TEAM, MSG, QN), BF16),
            pltpu.VMEM((4, MSG, QN), BF16),
            dma((9,)),
            dma((copies,)),
            dma((copies,)),
            dma((TEAM,)),
            dma((TEAM,)),
            dma((TEAM,)),
            dma((4,)),
        ],
        compiler_params=pltpu.CompilerParams(
            collective_id=0, has_side_effects=True, vmem_limit_bytes=60 * 1024 * 1024
        ),
    )(
        adapter_ids,
        block_order,
        queries.reshape(KV * QN, HD),
        features,
        jnp.swapaxes(adapter_down, 1, 2),
        adapter_key_up.reshape(-1, RANK * KV, HD),
        adapter_value_up.reshape(-1, RANK * KV, HD),
        base_key.reshape(-1, HD),
        base_value.reshape(-1, HD),
        prefix_key.reshape(-1, HD),
        prefix_value.reshape(-1, HD),
    )
    return result.reshape(QN, KV, 1, HD)


def solution(mesh):
    placed = (
        P("blk", "head", "team", None),
        P("blk", ("team", "head")),
        P(None, ("team", "head"), None),
        P(None, None, "head", None),
        P(None, None, "head", None),
        P("blk", "head", None),
        P("blk", "head", None),
        P("blk", "head", None),
        P("blk", "head", None),
        P(),
        P(),
    )
    return jax.shard_map(
        on_device,
        mesh=mesh,
        in_specs=placed,
        out_specs=P("blk", "head", "team", None),
        check_vma=False,
    )
```

```python
import math

import jax
import jax.numpy as jnp
from jax import lax
from jax.experimental import pallas as pl
from jax.experimental.pallas import tpu as pltpu
from jax.sharding import PartitionSpec as P

MESH = pl.DeviceIdType.MESH
BF16 = jnp.bfloat16
F32 = jnp.float32

TEAM, XN, YN = 8, 4, 4
QN, HD, KV = 256, 128, 2
PRE, NEW = 128, 64
PIECE = 2 * (PRE + NEW)
RANK, ADAPTERS = 64, 4
LOG_SCALE = math.log2(math.e) / math.sqrt(HD)
TAIL = 16
MSG = HD + TAIL
NT = (((1,), (1,)), ((), ()))
DIST = (4, 3, 5, 2, 6, 1, 7, 0)
COLUMNS = (0, 1, -1, 2)
FIRST = [(0, 0), (1, 0), (2, 0), (3, 0), (0, 1), (0, 3), (0, 2)]
SECOND = [(1, 1), (2, 1), (3, 1), (1, 3), (2, 3), (3, 3)]
LAST = [(1, 2), (2, 2), (3, 2)]
ALL = FIRST + SECOND + LAST
HALF = PRE // 2
EARLY = 12
SIZES = (
    len(FIRST) * PRE, len(SECOND) * HALF, len(SECOND) * HALF, EARLY * NEW,
    len(LAST) * PRE + (len(ALL) - EARLY) * NEW,
)
STARTS = tuple(sum(SIZES[:k]) for k in range(5))
KEYS = sum(SIZES)
NEW_KEY, NEW_VALUE = 0, 2 * HALF + NEW
PREFIX_AT = (NEW, 2 * NEW + 2 * HALF)
CUT = PREFIX_AT[1] - NEW // 2
PARTS = (pl.ds(0, CUT), pl.ds(CUT, PIECE - CUT))


def kernel(
    ids_ref, order_ref, q_hbm, feat_hbm, down_hbm, kup_hbm, vup_hbm, bk_hbm, bv_hbm, pk_hbm, pv_hbm,
    out_ref,
    q_ref, feat_ref, down_ref, up_ref, pre_ref, base_ref, wide, own_rows, ups, lat_part, lat_sib,
    lat_chip, lat_send, lat_team, lat_pair, lat_all, q_own, qbuf, kv, keys, values, vt, bias, scores,
    acc, tops, sent, from_sib, landed, local_sem, send_sem, recv_sem, core_send, core_recv, home_send, home_recv,
):
    team = lax.axis_index("team")
    blk = lax.axis_index("blk")
    head = lax.axis_index("head")
    yh, x = blk // XN, blk % XN
    ylo, core = head // 2, head % 2
    half, mine = team // 4, team % 2
    is_owner = (team % 4) // 2 == core
    not_owner = jnp.logical_not(is_owner)

    def at_z(d):
        return {"team": (team + d + TEAM) % TEAM}

    def at_blk(dy, dx):
        return {"blk": ((yh + dy + YN) % YN) * XN + (x + dx + XN) % XN}

    sibling = {"head": ylo * 2 + 1 - core}
    beside = {"head": (1 - ylo) * 2 + core}
    others = [(d, c) for d in range(YN) for c in range(XN) if (d, c) != (0, 0)]
    others.sort(key=lambda dc: -2 * min(dc[0], YN - dc[0]) - abs(COLUMNS[dc[1]]))

    barrier = pltpu.get_barrier_semaphore()
    by_z, by_blk = [at_z(d) for d in DIST[:-1]], [at_blk(d, COLUMNS[c]) for d, c in others]
    peers = by_blk[:4] + by_z[:3] + by_blk[4:10] + by_z[3:5] + by_blk[10:] + by_z[5:] + [beside, sibling]
    for peer in peers:
        pl.semaphore_signal(barrier, inc=1, device_id=peer, device_id_type=MESH)

    used = [0]

    def link(src, dst, peer):
        index = used[0]
        used[0] += 1
        return pltpu.make_async_remote_copy(
            src_ref=src, dst_ref=dst, send_sem=send_sem.at[index], recv_sem=recv_sem.at[index],
            device_id=peer, device_id_type=MESH,
        )

    pre_rows = pl.ds(pl.multiple_of(half * (KV * 2 * PRE), KV * 2 * PRE), KV * 2 * PRE)
    base_rows = pl.ds(pl.multiple_of(half * (KV * 2 * NEW), KV * 2 * NEW), KV * 2 * NEW)
    pairs = [
        (feat_hbm, feat_ref), (down_hbm, down_ref), (q_hbm, q_ref),
        (pk_hbm.at[pre_rows], pre_ref.at[0]), (pv_hbm.at[pre_rows], pre_ref.at[1]),
        (bk_hbm.at[base_rows], base_ref.at[0]), (bv_hbm.at[base_rows], base_ref.at[1]),
        (kup_hbm, up_ref.at[0]), (vup_hbm, up_ref.at[1]),
    ]
    local = [pltpu.make_async_copy(src, dst, local_sem.at[k]) for k, (src, dst) in enumerate(pairs)]
    for copy in local:
        copy.start()

    for copy in local[:2]:
        copy.wait()
    down = down_ref[ids_ref[blk]]
    partial = lax.dot_general(
        feat_ref[...], jnp.concatenate([down, down], axis=0), NT, preferred_element_type=F32
    )
    first_half = lax.broadcasted_iota(jnp.int32, (32, HD), 1) < RANK
    for quarter in range(4):
        row = quarter * NEW
        lat_part[quarter % 2, quarter // 2] = jnp.where(
            first_half, partial[row : row + 32], partial[row + 32 : row + 64]
        )

    for copy in local[2:]:
        copy.wait()
    wide[0 : KV * QN, :] = q_ref[...].astype(F32)
    for h in range(KV):
        q_own[h] = wide[pl.ds(h, QN, stride=2), :].astype(BF16)

    @pl.when(is_owner)
    def _():
        def pick(rows, count):
            wide[0 : 2 * count, :] = rows.astype(F32)
            even, odd = (wide[pl.ds(h, count, stride=2), :] for h in range(KV))
            return jnp.where(mine == 0, even, odd).astype(BF16)

        for kind in range(2):
            rows = pick(pre_ref[kind], 2 * PRE)
            fresh = pick(base_ref[kind], 2 * NEW)
            for c in range(2):
                at = NEW_VALUE if kind else NEW_KEY
                own_rows[c, at : at + NEW, :] = fresh[c * NEW : (c + 1) * NEW]
                for h in range(2):
                    at = PREFIX_AT[h] + kind * HALF
                    row = c * PRE + h * HALF
                    own_rows[c, at : at + HALF, :] = rows[row : row + HALF]
            for a in range(ADAPTERS):
                ups[a, :, kind * HD : (kind + 1) * HD] = pick(up_ref[kind, a], RANK)
        kv[0, 0] = own_rows[core]
        qbuf[3, QN:, :] = q_own[mine]

    pl.semaphore_wait(barrier, len(peers))

    def q_slot(i):
        return qbuf.at[i // 2, pl.ds((i % 2) * QN, QN)]

    lat_core = link(lat_part.at[1 - core], lat_sib, sibling)
    share_rows = link(own_rows.at[1 - core], kv.at[0, 0], sibling)
    share_ups = link(ups, ups, sibling)
    share_q = [link(q_slot(i), q_slot(i), sibling) for i in range(TEAM)]
    team_q = [
        link(q_own.at[(team + DIST[i]) % 2], q_slot(i), at_z(DIST[i])) for i in range(TEAM - 1)
    ]
    takes_q = [((team + DIST[i]) % 4) // 2 == core for i in range(TEAM - 1)]

    def rows_at(column, d, part):
        return kv.at[column, d, PARTS[part]]

    def along_y(column, d, part):
        copy = link(rows_at(column, 0, part), rows_at(column, d, part), at_blk(d, 0))
        copy.start()
        return copy

    def along_x(column, d, part):
        copy = link(rows_at(0, d, part), rows_at(column, d, part), at_blk(0, COLUMNS[column]))
        copy.start()
        return copy

    moved = {}

    def send_x(d, part):
        if d:
            moved[0, d, part].wait_recv()
        for c in (3, 1, 2):
            moved[c, d, part] = along_x(c, d, part)

    @pl.when(is_owner)
    def _():
        share_rows.start()

    lat_core.start()
    pl.when(takes_q[0])(team_q[0].start)

    @pl.when(not_owner)
    def _():
        share_rows.wait_recv()

    for d, part in ((1, 0), (3, 0), (1, 1), (3, 1), (2, 0), (2, 1)):
        moved[0, d, part] = along_y(0, d, part)
    send_x(0, 0)
    send_x(0, 1)

    lat_core.wait_recv()
    for h in range(2):
        total = lat_part[core, h] + lat_sib[h]
        lat_chip[h] = total
        lat_send[h] = total.astype(BF16)
    lat_z = [
        link(lat_send.at[((team + d) % TEAM) // 4], lat_team.at[d], at_z(d)) for d in DIST[:-1]
    ]
    for copy in lat_z:
        copy.start()
    for i in range(1, TEAM - 1):
        pl.when(takes_q[i])(team_q[i].start)

    @pl.when(is_owner)
    def _():
        share_ups.start()
        share_q[7].start()

    token = order_ref[blk] * QN + lax.broadcasted_iota(jnp.int32, (NEW, QN), 1)
    within = (2 * half + core) * NEW + lax.broadcasted_iota(jnp.int32, (NEW, QN), 0)

    def owner_of(column, d):
        return ((yh - d + YN) % YN) * XN + (x - COLUMNS[column] + XN) % XN

    for k, (column, d) in enumerate(ALL):
        hidden = order_ref[owner_of(column, d)] * QN + within > token
        bias[k * NEW : (k + 1) * NEW, :] = jnp.where(hidden, -1e30, 0.0)
    vt[HD:MSG, :] = jnp.ones((TAIL, KEYS), BF16)

    send_x(1, 0)
    send_x(3, 0)
    send_x(1, 1)
    send_x(3, 1)

    for copy in lat_z:
        copy.wait_recv()
    total = lat_chip[half]
    for d in range(1, TEAM):
        total = total + lat_team[d].astype(F32)
    lat_pair[0] = total
    lat_y = link(lat_pair.at[0], lat_pair.at[1], beside)
    lat_y.start()

    send_x(2, 0)
    lat_y.wait_recv()
    lat_all[0, 0] = (lat_pair[0] + lat_pair[1]).astype(BF16)
    lat_blk = {
        (c, d): link(lat_all.at[0, 0], lat_all.at[c, d], at_blk(d, COLUMNS[c])) for d, c in others
    }
    for copy in lat_blk.values():
        copy.start()

    send_x(2, 1)

    @pl.when(is_owner)
    def _():
        for i in (5, 6, 3, 4, 1, 2, 0):
            team_q[i].wait_recv()
            share_q[i].start()

    @pl.when(not_owner)
    def _():
        for i in range(TEAM):
            share_q[i].wait_recv()
        share_ups.wait_recv()

    def arrived(slots, part):
        for column, d in slots:
            pending = (column, d, part) in moved and (column, d, part) not in waited
            if pending:
                waited.add((column, d, part))
                moved[column, d, part].wait_recv()

    waited = {(0, d, part) for d in (1, 2, 3) for part in (0, 1)}

    def put_prefix(at, slots, part):
        row = PREFIX_AT[part]
        for k, (column, d) in enumerate(slots):
            to = at + k * HALF
            keys[to : to + HALF, :] = kv[column, d, row : row + HALF, :]
            values[to : to + HALF, :] = kv[column, d, row + HALF : row + 2 * HALF, :]

    def put_fresh(at, slot):
        packed = lat_all[slot[0], slot[1]].astype(F32)
        latent = jnp.concatenate(
            [jnp.where(first_half, packed, 0.0), jnp.where(first_half, 0.0, packed)], axis=0
        ).astype(BF16)
        up = ups[ids_ref[owner_of(*slot)]]
        delta = jnp.dot(latent, jnp.concatenate([up, up], axis=0), preferred_element_type=F32)
        new_key = kv[slot[0], slot[1], NEW_KEY : NEW_KEY + NEW, :].astype(F32)
        new_value = kv[slot[0], slot[1], NEW_VALUE : NEW_VALUE + NEW, :].astype(F32)
        keys[at : at + NEW, :] = (new_key + delta[:, 0:HD]).astype(BF16)
        values[at : at + NEW, :] = (new_value + delta[:, HD:]).astype(BF16)

    def turn(group):
        at, size = STARTS[group], SIZES[group]
        vt[0:HD, at : at + size] = values[at : at + size, :].T

    def score(group, k):
        at, size = STARTS[group], SIZES[group]
        s = lax.dot_general(keys[at : at + size, :], qbuf[k], NT, preferred_element_type=F32)
        first = 0 if group == 3 else len(LAST) * PRE if group == 4 else size
        if first < size:
            hide = bias[(0 if group == 3 else EARLY * NEW) :, :][: size - first]
            hide = s[first:] + jnp.concatenate([hide, hide], axis=1)
            s = jnp.concatenate([s[:first], hide], axis=0) if first else hide
        scores[k % 2, 0:size, :] = s
        top = jnp.max(s.reshape(size // 8, 8, 2 * QN), axis=0)
        top = jnp.max(top, axis=0, keepdims=True) * LOG_SCALE
        return top.astype(BF16).astype(F32)

    def weigh(group, k, top):
        at, size = STARTS[group], SIZES[group]
        if group:
            before = tops[k, 0:1, :]
            top = jnp.maximum(top, before)
        p = jnp.exp2(scores[k % 2, 0:size, :] * LOG_SCALE - top).astype(BF16)
        weighted = jnp.dot(vt[:, at : at + size], p, preferred_element_type=F32)
        if group:
            weighted = weighted + acc[k] * jnp.exp2(before - top)
        acc[k] = weighted
        tops[k] = jnp.broadcast_to(top, (8, 2 * QN))

    def run(group):
        top = score(group, 0)
        for k in range(TEAM // 2):
            ahead = score(group, k + 1) if k + 1 < TEAM // 2 else None
            weigh(group, k, top)
            top = ahead

    for part in range(2):
        arrived(FIRST, part)
        put_prefix(STARTS[0] + part * len(FIRST) * HALF, FIRST, part)
    turn(0)
    run(0)

    for part in range(2):
        arrived(SECOND, part)
        put_prefix(STARTS[1 + part], SECOND, part)
        turn(1 + part)
        run(1 + part)

    for copy in lat_blk.values():
        copy.wait_recv()
    for k, slot in enumerate(ALL[:EARLY]):
        put_fresh(STARTS[3] + k * NEW, slot)
    turn(3)
    run(3)

    for part in range(2):
        arrived(ALL[EARLY:], part)
    for part in range(2):
        put_prefix(STARTS[4] + part * len(LAST) * HALF, LAST, part)
    for k, slot in enumerate(ALL[EARLY:]):
        put_fresh(STARTS[4] + len(LAST) * PRE + k * NEW, slot)
    turn(4)

    tail_row = lax.broadcasted_iota(jnp.int32, (TAIL, QN), 0)

    def store(ref, state):
        weighted, row_sum, top = state
        ref[0:HD, :] = weighted.astype(BF16)
        high = row_sum.astype(BF16).astype(F32)
        tail = jnp.where(tail_row == 0, top, jnp.where(tail_row == 1, high, row_sum - high))
        ref[HD:MSG, :] = tail.astype(BF16)

    def held(i):
        side = slice((i % 2) * QN, (i % 2 + 1) * QN)
        return acc[i // 2, 0:HD, side], acc[i // 2, HD : HD + 1, side], tops[i // 2, 0:1, side]

    def read(ref):
        tail = ref[HD:MSG, :].astype(F32)
        return ref[0:HD, :].astype(F32), tail[1:2] + tail[2:3], tail[0:1]

    def merged(one, other):
        top = jnp.maximum(one[2], other[2])
        a, b = jnp.exp2(one[2] - top), jnp.exp2(other[2] - top)
        return one[0] * a + other[0] * b, one[1] * a + other[1] * b, top

    home_slot = mine * 2 + half

    def to_sibling(i):
        return pltpu.make_async_remote_copy(
            src_ref=sent.at[i], dst_ref=from_sib.at[i], send_sem=core_send.at[i], recv_sem=core_recv.at[i],
            device_id=sibling, device_id_type=MESH,
        )

    def homeward(i, slot):
        away = jnp.where(i % 2 == 0, 4 + i // 2, 4 - (i + 1) // 2)
        return pltpu.make_async_remote_copy(
            src_ref=sent.at[i], dst_ref=landed.at[slot], send_sem=home_send.at[i], recv_sem=home_recv.at[slot],
            device_id={"team": (team - away + TEAM) % TEAM}, device_id_type=MESH,
        )

    def merge_and_send(i):
        to_sibling(i).wait_recv()
        store(sent.at[i], merged(held(i), read(from_sib.at[i])))
        homeward(i, home_slot).start()

    top = score(4, 0)
    for k in range(TEAM // 2):
        ahead = score(4, k + 1) if k + 1 < TEAM // 2 else None
        weigh(4, k, top)
        top = ahead

        @pl.when(not_owner)
        def _():
            for i in (2 * k, 2 * k + 1):
                store(sent.at[i], held(i))
                to_sibling(i).start()

        if k:

            @pl.when(is_owner)
            def _():
                merge_and_send(2 * k - 2)
                merge_and_send(2 * k - 1)

    @pl.when(is_owner)
    def _():
        merge_and_send(6)
        to_sibling(7).wait_recv()
        store(landed.at[home_slot], merged(held(7), read(from_sib.at[7])))

    for h in range(KV):
        for part in range(2):
            slot = h * 2 + part

            @pl.when(team != part * 4 + core * 2 + h)
            def _():
                homeward(0, slot).wait_recv()

        weighted, row_sum, _ = merged(read(landed.at[h * 2]), read(landed.at[h * 2 + 1]))
        wide[pl.ds(h, QN, stride=2), :] = (weighted / row_sum).T
    out_ref[...] = wide[0 : KV * QN, :].astype(BF16)

    for copy in [lat_core, lat_y, *lat_z, *moved.values(), *lat_blk.values()]:
        copy.wait_send()
    for i in range(TEAM - 1):
        pl.when(takes_q[i])(team_q[i].wait_send)

    @pl.when(is_owner)
    def _():
        for copy in [share_rows, share_ups, *share_q]:
            copy.wait_send()

        def gone(i, carry):
            homeward(i, home_slot).wait_send()
            return carry

        lax.fori_loop(0, TEAM - 1, gone, 0)

    @pl.when(not_owner)
    def _():
        def gone(i, carry):
            to_sibling(i).wait_send()
            return carry

        lax.fori_loop(0, TEAM, gone, 0)


def on_device(
    queries, features, adapter_down, adapter_key_up, adapter_value_up,
    base_key, base_value, prefix_key, prefix_value, adapter_ids, block_order,
):
    copies = 1 + 1 + 1 + 8 + 7 + 7 + 1 + 15 + 30
    vmem = pl.BlockSpec(memory_space=pltpu.VMEM)
    smem = pl.BlockSpec(memory_space=pltpu.SMEM)
    hbm = pl.BlockSpec(memory_space=pl.ANY)
    dma = pltpu.SemaphoreType.DMA
    result = pl.pallas_call(
        kernel,
        out_shape=jax.ShapeDtypeStruct((KV * QN, HD), BF16),
        in_specs=[smem] * 2 + [hbm] * 9,
        out_specs=vmem,
        scratch_shapes=[
            pltpu.VMEM((KV * QN, HD), BF16),
            pltpu.VMEM(features.shape, BF16),
            pltpu.VMEM((ADAPTERS, RANK, features.shape[1]), BF16),
            pltpu.VMEM((2, ADAPTERS, KV * RANK, HD), BF16),
            pltpu.VMEM((2, KV * 2 * PRE, HD), BF16),
            pltpu.VMEM((2, KV * 2 * NEW, HD), BF16),
            pltpu.VMEM((KV * QN, HD), F32),
            pltpu.VMEM((2, PIECE, HD), BF16),
            pltpu.VMEM((ADAPTERS, RANK, 2 * HD), BF16),
            pltpu.VMEM((2, 2, 32, HD), F32),
            pltpu.VMEM((2, 32, HD), F32),
            pltpu.VMEM((2, 32, HD), F32),
            pltpu.VMEM((2, 32, HD), BF16),
            pltpu.VMEM((TEAM, 32, HD), BF16),
            pltpu.VMEM((2, 32, HD), F32),
            pltpu.VMEM((XN, YN, 32, HD), BF16),
            pltpu.VMEM((KV, QN, HD), BF16),
            pltpu.VMEM((TEAM // 2, 2 * QN, HD), BF16),
            pltpu.VMEM((XN, YN, PIECE, HD), BF16),
            pltpu.VMEM((KEYS, HD), BF16),
            pltpu.VMEM((KEYS, HD), BF16),
            pltpu.VMEM((MSG, KEYS), BF16),
            pltpu.VMEM((XN * YN * NEW, QN), F32),
            pltpu.VMEM((2, max(SIZES), 2 * QN), F32),
            pltpu.VMEM((TEAM // 2, MSG, 2 * QN), F32),
            pltpu.VMEM((TEAM // 2, 8, 2 * QN), F32),
            pltpu.VMEM((TEAM, MSG, QN), BF16),
            pltpu.VMEM((TEAM, MSG, QN), BF16),
            pltpu.VMEM((4, MSG, QN), BF16),
            dma((9,)),
            dma((copies,)),
            dma((copies,)),
            dma((TEAM,)),
            dma((TEAM,)),
            dma((TEAM,)),
            dma((4,)),
        ],
        compiler_params=pltpu.CompilerParams(
            collective_id=0, has_side_effects=True, vmem_limit_bytes=60 * 1024 * 1024
        ),
    )(
        adapter_ids,
        block_order,
        queries.reshape(KV * QN, HD),
        features,
        jnp.swapaxes(adapter_down, 1, 2),
        adapter_key_up.reshape(-1, RANK * KV, HD),
        adapter_value_up.reshape(-1, RANK * KV, HD),
        base_key.reshape(-1, HD),
        base_value.reshape(-1, HD),
        prefix_key.reshape(-1, HD),
        prefix_value.reshape(-1, HD),
    )
    return result.reshape(QN, KV, 1, HD)


def solution(mesh):
    placed = (
        P("blk", "head", "team", None),
        P("blk", ("team", "head")),
        P(None, ("team", "head"), None),
        P(None, None, "head", None),
        P(None, None, "head", None),
        P("blk", "head", None),
        P("blk", "head", None),
        P("blk", "head", None),
        P("blk", "head", None),
        P(),
        P(),
    )
    return jax.shard_map(
        on_device,
        mesh=mesh,
        in_specs=placed,
        out_specs=P("blk", "head", "team", None),
        check_vma=False,
    )
```

```python
import math

import jax
import jax.numpy as jnp
from jax import lax
from jax.experimental import pallas as pl
from jax.experimental.pallas import tpu as pltpu
from jax.sharding import PartitionSpec as P

MESH = pl.DeviceIdType.MESH
BF16 = jnp.bfloat16
F32 = jnp.float32

TEAM, XN, YN = 8, 4, 4
QN, HD, KV = 256, 128, 2
PRE, NEW = 128, 64
PIECE = 2 * (PRE + NEW)
RANK, ADAPTERS = 64, 4
LOG_SCALE = math.log2(math.e) / math.sqrt(HD)
TAIL = 16
MSG = HD + TAIL
NT = (((1,), (1,)), ((), ()))
DIST = (4, 3, 5, 2, 6, 1, 7, 0)
COLUMNS = (0, 1, -1, 2)
FIRST = [(0, 0), (1, 0), (2, 0), (3, 0), (0, 1), (0, 3), (0, 2)]
SECOND = [(1, 1), (2, 1), (3, 1), (1, 3), (2, 3), (3, 3)]
LAST = [(1, 2), (2, 2), (3, 2)]
ALL = FIRST + SECOND + LAST
HALF = PRE // 2
EARLY = 12
SIZES = (
    len(FIRST) * PRE, len(SECOND) * HALF, len(SECOND) * HALF, EARLY * NEW,
    len(LAST) * PRE + (len(ALL) - EARLY) * NEW,
)
STARTS = tuple(sum(SIZES[:k]) for k in range(5))
KEYS = sum(SIZES)
NEW_KEY, NEW_VALUE = 0, 2 * HALF + NEW
PREFIX_AT = (NEW, 2 * NEW + 2 * HALF)
CUT = PREFIX_AT[1] - NEW // 2
PARTS = (pl.ds(0, CUT), pl.ds(CUT, PIECE - CUT))


def kernel(
    ids_ref, order_ref, q_hbm, feat_hbm, down_hbm, kup_hbm, vup_hbm, bk_hbm, bv_hbm, pk_hbm, pv_hbm,
    out_ref,
    q_ref, feat_ref, down_ref, up_ref, pre_ref, base_ref, wide, own_rows, ups, lat_part, lat_sib,
    lat_chip, lat_team, lat_pair, lat_all, q_own, qbuf, kv, keys, values, vt, bias, scores,
    acc, tops, sent, from_sib, landed, local_sem, send_sem, recv_sem, core_send, core_recv, home_send, home_recv,
):
    team = lax.axis_index("team")
    blk = lax.axis_index("blk")
    head = lax.axis_index("head")
    yh, x = blk // XN, blk % XN
    ylo, core = head // 2, head % 2
    half, mine = team // 4, team % 2
    is_owner = (team % 4) // 2 == core
    not_owner = jnp.logical_not(is_owner)

    def at_z(d):
        return {"team": (team + d + TEAM) % TEAM}

    def at_blk(dy, dx):
        return {"blk": ((yh + dy + YN) % YN) * XN + (x + dx + XN) % XN}

    sibling = {"head": ylo * 2 + 1 - core}
    beside = {"head": (1 - ylo) * 2 + core}
    others = [(d, c) for d in range(YN) for c in range(XN) if (d, c) != (0, 0)]
    others.sort(key=lambda dc: -2 * min(dc[0], YN - dc[0]) - abs(COLUMNS[dc[1]]))

    barrier = pltpu.get_barrier_semaphore()
    by_z, by_blk = [at_z(d) for d in DIST[:-1]], [at_blk(d, COLUMNS[c]) for d, c in others]
    peers = by_blk[:4] + by_z[:3] + by_blk[4:10] + by_z[3:5] + by_blk[10:] + by_z[5:] + [beside, sibling]
    for peer in peers:
        pl.semaphore_signal(barrier, inc=1, device_id=peer, device_id_type=MESH)

    used = [0]

    def link(src, dst, peer):
        index = used[0]
        used[0] += 1
        return pltpu.make_async_remote_copy(
            src_ref=src, dst_ref=dst, send_sem=send_sem.at[index], recv_sem=recv_sem.at[index],
            device_id=peer, device_id_type=MESH,
        )

    pre_rows = pl.ds(pl.multiple_of(half * (KV * 2 * PRE), KV * 2 * PRE), KV * 2 * PRE)
    base_rows = pl.ds(pl.multiple_of(half * (KV * 2 * NEW), KV * 2 * NEW), KV * 2 * NEW)
    pairs = [
        (feat_hbm, feat_ref), (down_hbm, down_ref), (q_hbm, q_ref),
        (pk_hbm.at[pre_rows], pre_ref.at[0]), (pv_hbm.at[pre_rows], pre_ref.at[1]),
        (bk_hbm.at[base_rows], base_ref.at[0]), (bv_hbm.at[base_rows], base_ref.at[1]),
        (kup_hbm, up_ref.at[0]), (vup_hbm, up_ref.at[1]),
    ]
    local = [pltpu.make_async_copy(src, dst, local_sem.at[k]) for k, (src, dst) in enumerate(pairs)]
    for copy in local:
        copy.start()

    for copy in local[:2]:
        copy.wait()
    down = down_ref[ids_ref[blk]]
    partial = lax.dot_general(
        feat_ref[...], jnp.concatenate([down, down], axis=0), NT, preferred_element_type=F32
    )
    first_half = lax.broadcasted_iota(jnp.int32, (32, HD), 1) < RANK
    for quarter in range(4):
        row = quarter * NEW
        lat_part[quarter % 2, quarter // 2] = jnp.where(
            first_half, partial[row : row + 32], partial[row + 32 : row + 64]
        )

    for copy in local[2:]:
        copy.wait()
    wide[0 : KV * QN, :] = q_ref[...].astype(F32)
    for h in range(KV):
        q_own[h] = wide[pl.ds(h, QN, stride=2), :].astype(BF16)

    @pl.when(is_owner)
    def _():
        def pick(rows, count):
            wide[0 : 2 * count, :] = rows.astype(F32)
            even, odd = (wide[pl.ds(h, count, stride=2), :] for h in range(KV))
            return jnp.where(mine == 0, even, odd).astype(BF16)

        for kind in range(2):
            rows = pick(pre_ref[kind], 2 * PRE)
            fresh = pick(base_ref[kind], 2 * NEW)
            for c in range(2):
                at = NEW_VALUE if kind else NEW_KEY
                own_rows[c, at : at + NEW, :] = fresh[c * NEW : (c + 1) * NEW]
                for h in range(2):
                    at = PREFIX_AT[h] + kind * HALF
                    row = c * PRE + h * HALF
                    own_rows[c, at : at + HALF, :] = rows[row : row + HALF]
            for a in range(ADAPTERS):
                ups[a, :, kind * HD : (kind + 1) * HD] = pick(up_ref[kind, a], RANK)
        kv[0, 0] = own_rows[core]
        qbuf[3, QN:, :] = q_own[mine]

    pl.semaphore_wait(barrier, len(peers))

    def q_slot(i):
        return qbuf.at[i // 2, pl.ds((i % 2) * QN, QN)]

    lat_core = link(lat_part.at[1 - core], lat_sib, sibling)
    share_rows = link(own_rows.at[1 - core], kv.at[0, 0], sibling)
    share_ups = link(ups, ups, sibling)
    share_q = [link(q_slot(i), q_slot(i), sibling) for i in range(TEAM)]
    team_q = [
        link(q_own.at[(team + DIST[i]) % 2], q_slot(i), at_z(DIST[i])) for i in range(TEAM - 1)
    ]
    takes_q = [((team + DIST[i]) % 4) // 2 == core for i in range(TEAM - 1)]

    def rows_at(column, d, part):
        return kv.at[column, d, PARTS[part]]

    def along_y(column, d, part):
        copy = link(rows_at(column, 0, part), rows_at(column, d, part), at_blk(d, 0))
        copy.start()
        return copy

    def along_x(column, d, part):
        copy = link(rows_at(0, d, part), rows_at(column, d, part), at_blk(0, COLUMNS[column]))
        copy.start()
        return copy

    moved = {}

    def send_x(d, part):
        if d:
            moved[0, d, part].wait_recv()
        for c in (3, 1, 2):
            moved[c, d, part] = along_x(c, d, part)

    @pl.when(is_owner)
    def _():
        share_rows.start()

    lat_core.start()
    pl.when(takes_q[0])(team_q[0].start)

    @pl.when(not_owner)
    def _():
        share_rows.wait_recv()

    for d, part in ((1, 0), (3, 0), (1, 1), (3, 1), (2, 0), (2, 1)):
        moved[0, d, part] = along_y(0, d, part)
    send_x(0, 0)
    send_x(0, 1)

    lat_core.wait_recv()
    for h in range(2):
        lat_chip[h] = lat_part[core, h] + lat_sib[h]
    lat_z = [
        link(lat_chip.at[((team + d) % TEAM) // 4], lat_team.at[d], at_z(d)) for d in DIST[:-1]
    ]
    for copy in lat_z:
        copy.start()
    for i in range(1, TEAM - 1):
        pl.when(takes_q[i])(team_q[i].start)

    @pl.when(is_owner)
    def _():
        share_ups.start()
        share_q[7].start()

    token = order_ref[blk] * QN + lax.broadcasted_iota(jnp.int32, (NEW, QN), 1)
    within = (2 * half + core) * NEW + lax.broadcasted_iota(jnp.int32, (NEW, QN), 0)

    def owner_of(column, d):
        return ((yh - d + YN) % YN) * XN + (x - COLUMNS[column] + XN) % XN

    for k, (column, d) in enumerate(ALL):
        hidden = order_ref[owner_of(column, d)] * QN + within > token
        bias[k * NEW : (k + 1) * NEW, :] = jnp.where(hidden, -1e30, 0.0)
    vt[HD:MSG, :] = jnp.ones((TAIL, KEYS), BF16)

    send_x(1, 0)
    send_x(3, 0)
    send_x(1, 1)
    send_x(3, 1)

    for copy in lat_z:
        copy.wait_recv()
    total = lat_chip[half]
    for d in range(1, TEAM):
        total = total + lat_team[d]
    lat_pair[0] = total
    lat_y = link(lat_pair.at[0], lat_pair.at[1], beside)
    lat_y.start()

    send_x(2, 0)
    lat_y.wait_recv()
    lat_all[0, 0] = (lat_pair[0] + lat_pair[1]).astype(BF16)
    lat_blk = {
        (c, d): link(lat_all.at[0, 0], lat_all.at[c, d], at_blk(d, COLUMNS[c])) for d, c in others
    }
    for copy in lat_blk.values():
        copy.start()

    send_x(2, 1)

    @pl.when(is_owner)
    def _():
        for i in (5, 6, 3, 4, 1, 2, 0):
            team_q[i].wait_recv()
            share_q[i].start()

    @pl.when(not_owner)
    def _():
        for i in range(TEAM):
            share_q[i].wait_recv()
        share_ups.wait_recv()

    def arrived(slots, part):
        for column, d in slots:
            pending = (column, d, part) in moved and (column, d, part) not in waited
            if pending:
                waited.add((column, d, part))
                moved[column, d, part].wait_recv()

    waited = {(0, d, part) for d in (1, 2, 3) for part in (0, 1)}

    def put_prefix(at, slots, part):
        row = PREFIX_AT[part]
        for k, (column, d) in enumerate(slots):
            to = at + k * HALF
            keys[to : to + HALF, :] = kv[column, d, row : row + HALF, :]
            values[to : to + HALF, :] = kv[column, d, row + HALF : row + 2 * HALF, :]

    def put_fresh(at, slot):
        packed = lat_all[slot[0], slot[1]].astype(F32)
        latent = jnp.concatenate(
            [jnp.where(first_half, packed, 0.0), jnp.where(first_half, 0.0, packed)], axis=0
        ).astype(BF16)
        up = ups[ids_ref[owner_of(*slot)]]
        delta = jnp.dot(latent, jnp.concatenate([up, up], axis=0), preferred_element_type=F32)
        new_key = kv[slot[0], slot[1], NEW_KEY : NEW_KEY + NEW, :].astype(F32)
        new_value = kv[slot[0], slot[1], NEW_VALUE : NEW_VALUE + NEW, :].astype(F32)
        keys[at : at + NEW, :] = (new_key + delta[:, 0:HD]).astype(BF16)
        values[at : at + NEW, :] = (new_value + delta[:, HD:]).astype(BF16)

    def turn(group):
        at, size = STARTS[group], SIZES[group]
        vt[0:HD, at : at + size] = values[at : at + size, :].T

    def score(group, k):
        at, size = STARTS[group], SIZES[group]
        s = lax.dot_general(keys[at : at + size, :], qbuf[k], NT, preferred_element_type=F32)
        first = 0 if group == 3 else len(LAST) * PRE if group == 4 else size
        if first < size:
            hide = bias[(0 if group == 3 else EARLY * NEW) :, :][: size - first]
            hide = s[first:] + jnp.concatenate([hide, hide], axis=1)
            s = jnp.concatenate([s[:first], hide], axis=0) if first else hide
        scores[k % 2, 0:size, :] = s
        top = jnp.max(s.reshape(size // 8, 8, 2 * QN), axis=0)
        top = jnp.max(top, axis=0, keepdims=True) * LOG_SCALE
        return top.astype(BF16).astype(F32)

    def weigh(group, k, top):
        at, size = STARTS[group], SIZES[group]
        if group:
            before = tops[k, 0:1, :]
            top = jnp.maximum(top, before)
        p = jnp.exp2(scores[k % 2, 0:size, :] * LOG_SCALE - top).astype(BF16)
        weighted = jnp.dot(vt[:, at : at + size], p, preferred_element_type=F32)
        if group:
            weighted = weighted + acc[k] * jnp.exp2(before - top)
        acc[k] = weighted
        tops[k] = jnp.broadcast_to(top, (8, 2 * QN))

    def run(group):
        top = score(group, 0)
        for k in range(TEAM // 2):
            ahead = score(group, k + 1) if k + 1 < TEAM // 2 else None
            weigh(group, k, top)
            top = ahead

    for part in range(2):
        arrived(FIRST, part)
        put_prefix(STARTS[0] + part * len(FIRST) * HALF, FIRST, part)
    turn(0)
    run(0)

    for part in range(2):
        arrived(SECOND, part)
        put_prefix(STARTS[1 + part], SECOND, part)
        turn(1 + part)
        run(1 + part)

    for copy in lat_blk.values():
        copy.wait_recv()
    for k, slot in enumerate(ALL[:EARLY]):
        put_fresh(STARTS[3] + k * NEW, slot)
    turn(3)
    run(3)

    for part in range(2):
        arrived(ALL[EARLY:], part)
    for part in range(2):
        put_prefix(STARTS[4] + part * len(LAST) * HALF, LAST, part)
    for k, slot in enumerate(ALL[EARLY:]):
        put_fresh(STARTS[4] + len(LAST) * PRE + k * NEW, slot)
    turn(4)

    tail_row = lax.broadcasted_iota(jnp.int32, (TAIL, QN), 0)

    def store(ref, state):
        weighted, row_sum, top = state
        ref[0:HD, :] = weighted.astype(BF16)
        high = row_sum.astype(BF16).astype(F32)
        tail = jnp.where(tail_row == 0, top, jnp.where(tail_row == 1, high, row_sum - high))
        ref[HD:MSG, :] = tail.astype(BF16)

    def held(i):
        side = slice((i % 2) * QN, (i % 2 + 1) * QN)
        return acc[i // 2, 0:HD, side], acc[i // 2, HD : HD + 1, side], tops[i // 2, 0:1, side]

    def read(ref):
        tail = ref[HD:MSG, :].astype(F32)
        return ref[0:HD, :].astype(F32), tail[1:2] + tail[2:3], tail[0:1]

    def merged(one, other):
        top = jnp.maximum(one[2], other[2])
        a, b = jnp.exp2(one[2] - top), jnp.exp2(other[2] - top)
        return one[0] * a + other[0] * b, one[1] * a + other[1] * b, top

    home_slot = mine * 2 + half

    def to_sibling(i):
        return pltpu.make_async_remote_copy(
            src_ref=sent.at[i], dst_ref=from_sib.at[i], send_sem=core_send.at[i], recv_sem=core_recv.at[i],
            device_id=sibling, device_id_type=MESH,
        )

    def homeward(i, slot):
        away = jnp.where(i % 2 == 0, 4 + i // 2, 4 - (i + 1) // 2)
        return pltpu.make_async_remote_copy(
            src_ref=sent.at[i], dst_ref=landed.at[slot], send_sem=home_send.at[i], recv_sem=home_recv.at[slot],
            device_id={"team": (team - away + TEAM) % TEAM}, device_id_type=MESH,
        )

    def merge_and_send(i):
        to_sibling(i).wait_recv()
        store(sent.at[i], merged(held(i), read(from_sib.at[i])))
        homeward(i, home_slot).start()

    top = score(4, 0)
    for k in range(TEAM // 2):
        ahead = score(4, k + 1) if k + 1 < TEAM // 2 else None
        weigh(4, k, top)
        top = ahead

        @pl.when(not_owner)
        def _():
            for i in (2 * k, 2 * k + 1):
                store(sent.at[i], held(i))
                to_sibling(i).start()

        if k:

            @pl.when(is_owner)
            def _():
                merge_and_send(2 * k - 2)
                merge_and_send(2 * k - 1)

    @pl.when(is_owner)
    def _():
        merge_and_send(6)
        to_sibling(7).wait_recv()
        store(landed.at[home_slot], merged(held(7), read(from_sib.at[7])))

    for h in range(KV):
        for part in range(2):
            slot = h * 2 + part

            @pl.when(team != part * 4 + core * 2 + h)
            def _():
                homeward(0, slot).wait_recv()

        weighted, row_sum, _ = merged(read(landed.at[h * 2]), read(landed.at[h * 2 + 1]))
        wide[pl.ds(h, QN, stride=2), :] = (weighted / row_sum).T
    out_ref[...] = wide[0 : KV * QN, :].astype(BF16)

    for copy in [lat_core, lat_y, *lat_z, *moved.values(), *lat_blk.values()]:
        copy.wait_send()
    for i in range(TEAM - 1):
        pl.when(takes_q[i])(team_q[i].wait_send)

    @pl.when(is_owner)
    def _():
        for copy in [share_rows, share_ups, *share_q]:
            copy.wait_send()

        def gone(i, carry):
            homeward(i, home_slot).wait_send()
            return carry

        lax.fori_loop(0, TEAM - 1, gone, 0)

    @pl.when(not_owner)
    def _():
        def gone(i, carry):
            to_sibling(i).wait_send()
            return carry

        lax.fori_loop(0, TEAM, gone, 0)


def on_device(
    queries, features, adapter_down, adapter_key_up, adapter_value_up,
    base_key, base_value, prefix_key, prefix_value, adapter_ids, block_order,
):
    copies = 1 + 1 + 1 + 8 + 7 + 7 + 1 + 15 + 30
    vmem = pl.BlockSpec(memory_space=pltpu.VMEM)
    smem = pl.BlockSpec(memory_space=pltpu.SMEM)
    hbm = pl.BlockSpec(memory_space=pl.ANY)
    dma = pltpu.SemaphoreType.DMA
    result = pl.pallas_call(
        kernel,
        out_shape=jax.ShapeDtypeStruct((KV * QN, HD), BF16),
        in_specs=[smem] * 2 + [hbm] * 9,
        out_specs=vmem,
        scratch_shapes=[
            pltpu.VMEM((KV * QN, HD), BF16),
            pltpu.VMEM(features.shape, BF16),
            pltpu.VMEM((ADAPTERS, RANK, features.shape[1]), BF16),
            pltpu.VMEM((2, ADAPTERS, KV * RANK, HD), BF16),
            pltpu.VMEM((2, KV * 2 * PRE, HD), BF16),
            pltpu.VMEM((2, KV * 2 * NEW, HD), BF16),
            pltpu.VMEM((KV * QN, HD), F32),
            pltpu.VMEM((2, PIECE, HD), BF16),
            pltpu.VMEM((ADAPTERS, RANK, 2 * HD), BF16),
            pltpu.VMEM((2, 2, 32, HD), F32),
            pltpu.VMEM((2, 32, HD), F32),
            pltpu.VMEM((2, 32, HD), F32),
            pltpu.VMEM((TEAM, 32, HD), F32),
            pltpu.VMEM((2, 32, HD), F32),
            pltpu.VMEM((XN, YN, 32, HD), BF16),
            pltpu.VMEM((KV, QN, HD), BF16),
            pltpu.VMEM((TEAM // 2, 2 * QN, HD), BF16),
            pltpu.VMEM((XN, YN, PIECE, HD), BF16),
            pltpu.VMEM((KEYS, HD), BF16),
            pltpu.VMEM((KEYS, HD), BF16),
            pltpu.VMEM((MSG, KEYS), BF16),
            pltpu.VMEM((XN * YN * NEW, QN), F32),
            pltpu.VMEM((2, max(SIZES), 2 * QN), F32),
            pltpu.VMEM((TEAM // 2, MSG, 2 * QN), F32),
            pltpu.VMEM((TEAM // 2, 8, 2 * QN), F32),
            pltpu.VMEM((TEAM, MSG, QN), BF16),
            pltpu.VMEM((TEAM, MSG, QN), BF16),
            pltpu.VMEM((4, MSG, QN), BF16),
            dma((9,)),
            dma((copies,)),
            dma((copies,)),
            dma((TEAM,)),
            dma((TEAM,)),
            dma((TEAM,)),
            dma((4,)),
        ],
        compiler_params=pltpu.CompilerParams(
            collective_id=0, has_side_effects=True, vmem_limit_bytes=60 * 1024 * 1024
        ),
    )(
        adapter_ids,
        block_order,
        queries.reshape(KV * QN, HD),
        features,
        jnp.swapaxes(adapter_down, 1, 2),
        adapter_key_up.reshape(-1, RANK * KV, HD),
        adapter_value_up.reshape(-1, RANK * KV, HD),
        base_key.reshape(-1, HD),
        base_value.reshape(-1, HD),
        prefix_key.reshape(-1, HD),
        prefix_value.reshape(-1, HD),
    )
    return result.reshape(QN, KV, 1, HD)


def solution(mesh):
    placed = (
        P("blk", "head", "team", None),
        P("blk", ("team", "head")),
        P(None, ("team", "head"), None),
        P(None, None, "head", None),
        P(None, None, "head", None),
        P("blk", "head", None),
        P("blk", "head", None),
        P("blk", "head", None),
        P("blk", "head", None),
        P(),
        P(),
    )
    return jax.shard_map(
        on_device,
        mesh=mesh,
        in_specs=placed,
        out_specs=P("blk", "head", "team", None),
        check_vma=False,
    )
```
